128 devices in a mesh: tm: 8 (over y, core), seq: 16 (over x, z).
Axes of the slice: x: 4, y: 4, z: 4, core: 2. Of those that a mesh axis runs over, the one named last changes fastest.
Arguments:
- queries: bfloat16 [8, 4096, 2048], P('tm', 'seq'), may hold values from -6 to 6
- keys: bfloat16 [8, 4480, 2048], P('tm', 'seq'), may hold values from -6 to 6
- values: bfloat16 [8, 4480, 2048], P('tm', 'seq'), may hold values from -6 to 6
- hidden: bfloat16 [8, 4096, 2432], P('tm', 'seq'), may hold values from -0.119628906 to 0.119628906
- w_proj: bfloat16 [2048, 2432], replicated, may hold values from -0.125 to 0.125
- w_final: bfloat16 [2432, 64], replicated, may hold values from -0.125 to 0.125
- gate_base: float32 [2432], replicated, may hold values from -6 to 6
- gate_slope: float32 [2432], replicated, may hold values from -6 to 6
- start_latent: float32 [4096, 64], P('seq'), may hold values from -6 to 6
- window_steps: int32 [9], replicated, may hold values from 0 to 16, as said below
Outputs:
- velocity: float32 [8, 4096, 64], P('tm', 'seq')
- latents: float32 [8, 4096, 64], P('tm', 'seq')
The draws below stay inside these ranges and needn't reach their ends.
Inputs may be any that keep to these rules, and one draw needn't show every extreme that they name: window_steps[0] is 0, the last entry is 16, and each entry exceeds the one before by 1 to 3.
All inputs are finite; a program needn't handle non-finite values.
Results may differ from the reference program's by a relative error of at most 0.0059.
Values may be sent and summed in bfloat16 or wider, within the bound.
No kernel may reach another device: no remote copies, remote signals or barrier semaphores. Data moves between devices by JAX's collectives and lax.ppermute only.
A program may use at most 192 MiB of HBM per device.

```python
import jax
import jax.numpy as jnp
from jax import lax

D = 2432
HEADS = 32
HEAD_DIM = 64
LAT = 64
HD = 2048
KEYS = 4480
IMG = 4096
TIMES = 8
STEPS = 16


def draw_window_steps(key, part):
    key = jax.random.fold_in(key, 7)
    pair_key = jax.random.fold_in(key, 1)
    order_key = jax.random.fold_in(key, 2)
    picks = jax.random.randint(pair_key, (TIMES // 2,), 0, 3)
    first = jnp.where(picks == 0, 2, jnp.where(picks == 1, 1, 3)).astype(jnp.int32)
    second = (4 - first).astype(jnp.int32)
    strides = jnp.concatenate([first, second])
    strides = jax.random.permutation(order_key, strides)
    return jnp.concatenate([jnp.zeros((1,), jnp.int32), jnp.cumsum(strides).astype(jnp.int32)])


def block_levels(own_key, shape, pieces, least, high):
    factor_of, own = 1.0, jax.random.fold_in(own_key, 6)
    for dim, blocks in pieces:
        heights = jnp.exp(jax.random.uniform(jax.random.fold_in(own, dim), (blocks,), jnp.float32, least / len(pieces), high / len(pieces)))
        factor_of = factor_of * jnp.repeat(heights, shape[dim] // blocks).reshape([-1 if axis == dim else 1 for axis in range(len(shape))])
    return factor_of


def noise(key, extent, spread, most, shards=(), dtype=jnp.bfloat16):
    array = jax.random.normal(key, extent, jnp.float32) * spread
    if len(shards) > 0:
        array = block_levels(key, extent, shards, -0.22, 0.18) * array
    return jnp.clip(array, min=-most, max=most).astype(dtype)


def setup_inputs(seed: int = 0) -> dict:
    key_list = jax.random.split(jax.random.key(seed), 11)
    queries = noise(key_list[0], (TIMES, IMG, HD), 1.0, 6.0, ((0, 8), (1, 16)))
    keys = noise(key_list[1], (TIMES, KEYS, HD), 1.0, 6.0, ((0, 8), (1, 16)))
    values = noise(key_list[2], (TIMES, KEYS, HD), 1.0, 6.0, ((0, 8), (1, 16)))
    hidden = noise(key_list[3], (TIMES, IMG, D), 0.02, 0.119628906, ((0, 8), (1, 16)))
    w_proj = noise(key_list[4], (HD, D), HD ** -0.5, 0.125)
    w_final = noise(key_list[5], (D, LAT), D ** -0.5, 0.125)
    gate_base = noise(key_list[6], (D,), 1.0, 6.0, (), jnp.float32)
    gate_slope = noise(key_list[7], (D,), 1.0, 6.0, (), jnp.float32)
    start_latent = noise(key_list[8], (IMG, LAT), 1.0, 6.0, ((0, 16),), jnp.float32)
    window_steps = draw_window_steps(jax.random.fold_in(key_list[10], 71), 0)
    return {"queries": queries, "keys": keys, "values": values, "hidden": hidden, "w_proj": w_proj, "w_final": w_final, "gate_base": gate_base, "gate_slope": gate_slope, "start_latent": start_latent, "window_steps": window_steps}


def head_norm(tensor_in):
    count = tensor_in.shape[0]
    values_f = tensor_in.astype(jnp.float32).reshape(count, HEADS, HEAD_DIM)
    scaled = values_f * lax.rsqrt(lax.optimization_barrier(jnp.mean(values_f * values_f, axis=-1, keepdims=True)) + 1e-06)
    return scaled.astype(jnp.bfloat16)

def sigma_of(index_val):
    frac = 1.0 - index_val.astype(jnp.float32) / STEPS
    return 3.0 * frac / (1.0 + 2.0 * frac)

def head_attend(operands):
    query_head, key_head, value_head = operands
    scores = jnp.dot(query_head, key_head.T, preferred_element_type=jnp.float32) * 0.125
    weights = jnp.exp(scores)
    totals = lax.optimization_barrier(jnp.sum(weights, axis=1))
    summed = jnp.dot(weights.astype(jnp.bfloat16), value_head, preferred_element_type=jnp.float32)
    return summed / totals[:, None]

def velocity_one(operands, w_proj, w_final, gate_base, gate_slope):
    query_t, key_t, value_t, hidden_t, sigma_t = operands
    query_heads = head_norm(query_t).transpose(1, 0, 2)
    key_heads = head_norm(key_t).transpose(1, 0, 2)
    value_heads = value_t.reshape(-1, HEADS, HEAD_DIM).transpose(1, 0, 2)
    attended = lax.map(head_attend, (query_heads, key_heads, value_heads))
    attended = attended.transpose(1, 0, 2).reshape(query_t.shape[0], HD).astype(jnp.bfloat16)
    projected = jnp.dot(attended, w_proj, preferred_element_type=jnp.float32)
    gated = hidden_t.astype(jnp.float32) + (gate_base + sigma_t * gate_slope) * projected
    normed = (gated * lax.rsqrt(lax.optimization_barrier(jnp.mean(gated * gated, axis=-1, keepdims=True)) + 1e-06)).astype(jnp.bfloat16)
    return jnp.dot(normed, w_final, preferred_element_type=jnp.float32)

def reference(queries, keys, values, hidden, w_proj, w_final, gate_base, gate_slope, start_latent, window_steps):
    sigmas = sigma_of(window_steps)
    step_sizes = sigmas[1:] - sigmas[:-1]
    velocity = lax.map(lambda operands: velocity_one(operands, w_proj, w_final, gate_base, gate_slope), (queries, keys, values, hidden, sigmas[:-1]))
    drift = step_sizes[:, None, None] * velocity
    latents = start_latent[None] + jnp.cumsum(drift, axis=0)
    return (velocity, latents)
```

```python
import functools

import jax
import jax.numpy as jnp
from jax import lax
from jax.experimental import pallas as pl
from jax.experimental.pallas import tpu as pltpu
from jax.sharding import PartitionSpec as P

HEADS = 32
HEAD_DIM = 64
HD = 2048
D = 2432
LAT = 64
PAIR = 128
RING = 4
BOTH = ("tm", "seq")
NT = (((1,), (1,)), ((), ()))
SCALE = 0.125 * 1.4426950408889634
KEY_CUTS = ((0, 144), (144, 280))
PIECES = ((0, 128), (128, 256))
QROWS = 256
TILE = 512
BLOCK_Q = 1024
VROWS = 128
MIB = 2**20


def ring_perm(first, shift):
    pairs = []
    for slot in range(8):
        for place in range(16):
            x, z = divmod(place, RING)
            if (slot % 2 == 0) == first:
                x2, z2 = (x + shift) % RING, z
            else:
                x2, z2 = x, (z + shift) % RING
            pairs.append((slot * 16 + place, slot * 16 + x2 * RING + z2))
    return pairs


def send(value, first, shift):
    return lax.ppermute(value, BOTH, ring_perm(first, shift % RING))


def head_norm(block):
    wide = block.astype(jnp.float32)
    square = wide * wide
    high = square.astype(jnp.bfloat16)
    low = (square - high.astype(jnp.float32)).astype(jnp.bfloat16)
    row = lax.broadcasted_iota(jnp.int32, (PAIR, PAIR), 0)
    col = lax.broadcasted_iota(jnp.int32, (PAIR, PAIR), 1)
    same = ((row < HEAD_DIM) == (col < HEAD_DIM)).astype(jnp.bfloat16)
    total = jnp.dot(high, same, preferred_element_type=jnp.float32)
    total = total + jnp.dot(low, same, preferred_element_type=jnp.float32)
    return (wide * lax.rsqrt(total * (1.0 / HEAD_DIM) + 1e-06)).astype(jnp.bfloat16)


def padded(rows):
    return -(-rows // 16) * 16


def pack_kernel(nq, cut, place_ref, *refs):
    if nq:
        q_ref, k_ref, v_ref = refs[:3]
        outs = refs[3:]
    else:
        k_ref, v_ref = refs[:2]
        outs = refs[2:]
    k0, k1 = cut
    nk = k1 - k0
    kp = nq
    vp = kp + padded(nk)
    for d in range(RING):
        group = lax.rem(place_ref[0] + d, RING)
        for j in range(RING):
            lanes = pl.ds(pl.multiple_of(group * (RING * PAIR) + j * PAIR, PAIR), PAIR)
            out = outs[d]
            if nq:
                out[j, 0:nq] = head_norm(q_ref[:, lanes])
            out[j, kp : kp + nk] = head_norm(k_ref[k0:k1, lanes])
            out[j, vp : vp + nk] = v_ref[k0:k1, lanes]
            if vp > kp + nk:
                out[j, kp + nk : vp] = jnp.zeros((vp - kp - nk, PAIR), jnp.bfloat16)


def pack(place, queries, keys, values, nq, cut):
    nk = cut[1] - cut[0]
    rows = nq + padded(nk) + nk
    operands = ([queries] if nq else []) + [keys, values]
    vmem = pl.BlockSpec(memory_space=pltpu.VMEM)
    return pl.pallas_call(
        functools.partial(pack_kernel, nq, cut),
        in_specs=[pl.BlockSpec(memory_space=pltpu.SMEM)] + [vmem] * len(operands),
        out_specs=[vmem] * RING,
        out_shape=[jax.ShapeDtypeStruct((RING, rows, PAIR), jnp.bfloat16)] * RING,
        compiler_params=pltpu.CompilerParams(vmem_limit_bytes=16 * MIB),
        cost_estimate=pl.CostEstimate(flops=2 * 2 * rows * HD * PAIR, bytes_accessed=4 * rows * HD, transcendentals=0),
        name="pack",
    )(place, *operands)


def regroup(parts, index):
    return [
        jnp.stack([lax.dynamic_index_in_dim(part, lax.rem(index + e, RING), 0, keepdims=False) for part in parts])
        for e in range(RING)
    ]


def exchange(parts, second):
    landed = [parts[0]] + [send(parts[d], True, d) for d in range(1, RING)]
    staged = regroup(landed, second)
    return [staged[0]] + [send(staged[e], False, e) for e in range(1, RING)]


def give_back(blocks):
    landed = [blocks[0]] + [send(blocks[e], False, -e) for e in range(1, RING)]
    staged = [jnp.stack([block[d] for block in landed]) for d in range(RING)]
    return [staged[0]] + [send(staged[d], True, -d) for d in range(1, RING)]


def cuts_of(total, step):
    return [(start, min(step, total - start)) for start in range(0, total, step)]


def attend_kernel(nk, kp, rows, first, last, *refs):
    q_refs, refs = refs[:RING], refs[RING:]
    if first:
        kv_refs = q_refs
    else:
        kv_refs, refs = refs[:RING], refs[RING:]
        acc_in, refs = refs[0], refs[1:]
    if last:
        out_refs, refs = refs[:RING], refs[RING:]
    else:
        acc_out, refs = refs[0], refs[1:]
    q_all, k_all, low_t, high_t = refs
    vp = kp + padded(nk)
    r0, r1 = rows
    nr = r1 - r0
    total = RING * RING * nk
    row = lax.broadcasted_iota(jnp.int32, (PAIR, PAIR), 0)
    col = lax.broadcasted_iota(jnp.int32, (PAIR, PAIR), 1)
    eye = (row == col).astype(jnp.bfloat16)
    for e in range(RING):
        for d in range(RING):
            slot = e * RING + d
            for p0, p1 in PIECES:
                if r0 <= p0 and p1 <= r1:
                    base = RING * RING * (p0 - r0) + slot * (p1 - p0)
                    q_all[base : base + p1 - p0] = q_refs[e][d, p0:p1]
            k_all[slot * nk : (slot + 1) * nk] = kv_refs[e][d, kp : kp + nk]
    ones = jnp.ones((VROWS - HEAD_DIM, total), jnp.bfloat16)
    low_t[HEAD_DIM:, :] = ones
    high_t[HEAD_DIM:, :] = ones
    for e in range(RING):
        joined = jnp.concatenate([kv_refs[e][d, vp : vp + nk] for d in range(RING)], axis=0)
        turned = lax.dot_general(eye, joined, NT, preferred_element_type=jnp.float32).astype(jnp.bfloat16)
        low_t[0:HEAD_DIM, e * RING * nk : (e + 1) * RING * nk] = turned[:HEAD_DIM]
        high_t[0:HEAD_DIM, e * RING * nk : (e + 1) * RING * nk] = turned[HEAD_DIM:]
    values_t = (low_t, high_t)
    work = [(h, start, size) for start, size in cuts_of(total, TILE) for h in range(2)]

    @pl.loop(0, RING * RING * nr // BLOCK_Q)
    def _(block):
        q0 = pl.multiple_of(block * BLOCK_Q, BLOCK_Q)
        q = q_all[pl.ds(q0, BLOCK_Q), :]
        lane = lax.broadcasted_iota(jnp.int32, q.shape, 1)
        zero = jnp.zeros_like(q)
        halves = (jnp.where(lane < HEAD_DIM, q, zero), jnp.where(lane < HEAD_DIM, zero, q))
        sums = [jnp.zeros((VROWS, BLOCK_Q), jnp.float32) for _ in range(2)]

        def score(item):
            h, start, size = item
            return lax.dot_general(k_all[start : start + size, :], halves[h], NT, preferred_element_type=jnp.float32)

        ahead = score(work[0])
        for i, (h, start, size) in enumerate(work):
            now = ahead
            if i + 1 < len(work):
                ahead = score(work[i + 1])
            weights = jnp.exp2(now * SCALE).astype(jnp.bfloat16)
            sums[h] = sums[h] + jnp.dot(
                values_t[h][:, start : start + size], weights, preferred_element_type=jnp.float32
            )
        kept = HEAD_DIM + 8
        if not first:
            qa = pl.multiple_of(RING * RING * r0 + block * BLOCK_Q, BLOCK_Q)
            sums = [sums[h][:kept] + acc_in[h, :, pl.ds(qa, BLOCK_Q)] for h in range(2)]
        if not last:
            for h in range(2):
                acc_out[h, :, pl.ds(q0, BLOCK_Q)] = sums[h][:kept]
        else:
            done = jnp.concatenate([s[:HEAD_DIM] / s[HEAD_DIM : HEAD_DIM + 1] for s in sums], axis=0)
            q_all[pl.ds(q0, BLOCK_Q), :] = done.T.astype(jnp.bfloat16)

    if last:
        for e in range(RING):
            for d in range(RING):
                slot = e * RING + d
                out_refs[e][d] = q_all[slot * nr : (slot + 1) * nr]


def attend(q_parts, kv_parts, acc, nk, kp, rows, last):
    first = acc is None
    nr = rows[1] - rows[0]
    nq = RING * RING * nr
    total = RING * RING * nk
    operands = list(q_parts) + ([] if first else list(kv_parts) + [acc])
    vmem = pl.BlockSpec(memory_space=pltpu.VMEM)
    if last:
        out_shape = [jax.ShapeDtypeStruct((RING, nr, PAIR), jnp.bfloat16)] * RING
    else:
        out_shape = [jax.ShapeDtypeStruct((2, HEAD_DIM + 8, nq), jnp.float32)]
    return pl.pallas_call(
        functools.partial(attend_kernel, nk, kp, rows, first, last),
        in_specs=[vmem] * len(operands),
        out_specs=[vmem] * len(out_shape),
        out_shape=out_shape,
        scratch_shapes=[
            pltpu.VMEM((nq, PAIR), jnp.bfloat16),
            pltpu.VMEM((total, PAIR), jnp.bfloat16),
            pltpu.VMEM((VROWS, total), jnp.bfloat16),
            pltpu.VMEM((VROWS, total), jnp.bfloat16),
        ],
        compiler_params=pltpu.CompilerParams(vmem_limit_bytes=32 * MIB),
        cost_estimate=pl.CostEstimate(
            flops=2 * 2 * 4 * nq * total * PAIR, bytes_accessed=2 * MIB, transcendentals=2 * nq * total
        ),
        name="attend",
    )(*operands)


def project_kernel(rows, place_ref, level_ref, *refs):
    parts, refs = refs[:RING], refs[RING:]
    hidden_ref, w_proj_ref, w_final_ref, base_ref, slope_ref, out_ref, joined, gated = refs
    r0, r1 = rows
    for d in range(RING):
        for e in range(RING):
            pair = lax.rem(place_ref[0] + d, RING) * RING + lax.rem(place_ref[1] + e, RING)
            joined[:, pl.ds(pl.multiple_of(pair * PAIR, PAIR), PAIR)] = parts[d][e]
    squares = jnp.zeros((r1 - r0, 1), jnp.float32)
    for start, size in cuts_of(D, 512):
        cols = slice(start, start + size)
        projected = jnp.dot(joined[...], w_proj_ref[:, cols], preferred_element_type=jnp.float32)
        gate = base_ref[:, cols] + level_ref[0] * slope_ref[:, cols]
        value = hidden_ref[r0:r1, cols].astype(jnp.float32) + gate * projected
        gated[:, cols] = value
        squares = squares + jnp.sum(value * value, axis=1, keepdims=True)
    normed = (gated[...] * lax.rsqrt(squares * (1.0 / D) + 1e-06)).astype(jnp.bfloat16)
    out_ref[...] = jnp.dot(normed, w_final_ref[...], preferred_element_type=jnp.float32)


def project(place, level, parts, hidden, w_proj, w_final, base, slope, rows):
    nr = rows[1] - rows[0]
    vmem = pl.BlockSpec(memory_space=pltpu.VMEM)
    smem = pl.BlockSpec(memory_space=pltpu.SMEM)
    return pl.pallas_call(
        functools.partial(project_kernel, rows),
        in_specs=[smem, smem] + [vmem] * (RING + 5),
        out_specs=vmem,
        out_shape=jax.ShapeDtypeStruct((nr, LAT), jnp.float32),
        scratch_shapes=[pltpu.VMEM((nr, HD), jnp.bfloat16), pltpu.VMEM((nr, D), jnp.float32)],
        compiler_params=pltpu.CompilerParams(vmem_limit_bytes=32 * MIB),
        cost_estimate=pl.CostEstimate(flops=2 * nr * HD * D, bytes_accessed=12 * MIB, transcendentals=0),
        name="project",
    )(place, level, *parts, hidden, w_proj, w_final, base, slope)


def sigma_of(index_val, total_steps):
    frac = 1.0 - index_val.astype(jnp.float32) / total_steps
    return 3.0 * frac / (1.0 + 2.0 * frac)


def running_sum(drift, slots):
    shift = 1
    while shift < slots:
        drift = drift + lax.ppermute(drift, "tm", [(i, i + shift) for i in range(slots - shift)])
        shift *= 2
    return drift


def per_device(
    queries, keys, values, hidden, w_proj, w_final, gate_base, gate_slope, start_latent, window_steps
):
    slots = lax.axis_size("tm")
    slot = lax.axis_index("tm")
    seat = lax.axis_index("seq")
    x, z = seat // RING, lax.rem(seat, RING)
    even = lax.rem(slot, 2) == 0
    first, second = jnp.where(even, x, z), jnp.where(even, z, x)
    place = jnp.stack([first, second]).astype(jnp.int32)
    sigma_now = sigma_of(window_steps[slot], 2 * slots)
    step_size = sigma_of(window_steps[slot + 1], 2 * slots) - sigma_now
    level = sigma_now.reshape(1)

    received = []
    for number, cut in enumerate(KEY_CUTS):
        parts = pack(place, queries[0], keys[0], values[0], QROWS if number == 0 else 0, cut)
        received.append(exchange(parts, second))
    q_parts = received[0]
    acc = None
    outs = []
    for number, cut in enumerate(KEY_CUTS):
        nk = cut[1] - cut[0]
        kp = QROWS if number == 0 else 0
        if number < len(KEY_CUTS) - 1:
            (acc,) = attend(q_parts, received[number], acc, nk, kp, (0, QROWS), False)
        else:
            outs = [attend(q_parts, received[number], acc, nk, kp, rows, True) for rows in PIECES]
    velocities, latents = [], []
    for rows, blocks in zip(PIECES, outs):
        back = give_back(blocks)
        velocity = project(
            place, level, back, hidden[0], w_proj, w_final, gate_base[None], gate_slope[None], rows
        )
        velocities.append(velocity)
        latents.append(start_latent[rows[0] : rows[1]] + running_sum(step_size * velocity, slots))
    return (jnp.concatenate(velocities)[None], jnp.concatenate(latents)[None])


def solution(mesh):
    placed = (
        P("tm", "seq", None),
        P("tm", "seq", None),
        P("tm", "seq", None),
        P("tm", "seq", None),
        P(),
        P(),
        P(),
        P(),
        P("seq", None),
        P(),
    )
    return jax.shard_map(
        per_device,
        mesh=mesh,
        in_specs=placed,
        out_specs=(P("tm", "seq", None), P("tm", "seq", None)),
        check_vma=False,
    )
```

```python
import functools

import jax
import jax.numpy as jnp
from jax import lax
from jax.experimental import pallas as pl
from jax.experimental.pallas import tpu as pltpu
from jax.sharding import PartitionSpec as P

HEADS = 32
HEAD_DIM = 64
HD = 2048
D = 2432
LAT = 64
PAIR = 128
RING = 4
BOTH = ("tm", "seq")
NT = (((1,), (1,)), ((), ()))
SCALE = 0.125 * 1.4426950408889634
KEY_CUTS = ((0, 96), (96, 280))
QROWS = 256
KROWS = 280
TILE = 512
BLOCK_Q = 1024
VROWS = 128
MIB = 2**20


def ring_perm(first, shift):
    pairs = []
    for slot in range(8):
        for place in range(16):
            x, z = divmod(place, RING)
            if (slot % 2 == 0) == first:
                x2, z2 = (x + shift) % RING, z
            else:
                x2, z2 = x, (z + shift) % RING
            pairs.append((slot * 16 + place, slot * 16 + x2 * RING + z2))
    return pairs


def send(value, first, shift):
    return lax.ppermute(value, BOTH, ring_perm(first, shift % RING))


def head_norm(block):
    wide = block.astype(jnp.float32)
    square = wide * wide
    high = square.astype(jnp.bfloat16)
    low = (square - high.astype(jnp.float32)).astype(jnp.bfloat16)
    row = lax.broadcasted_iota(jnp.int32, (PAIR, PAIR), 0)
    col = lax.broadcasted_iota(jnp.int32, (PAIR, PAIR), 1)
    same = ((row < HEAD_DIM) == (col < HEAD_DIM)).astype(jnp.bfloat16)
    total = jnp.dot(high, same, preferred_element_type=jnp.float32)
    total = total + jnp.dot(low, same, preferred_element_type=jnp.float32)
    return (wide * lax.rsqrt(total * (1.0 / HEAD_DIM) + 1e-06)).astype(jnp.bfloat16)


def padded(rows):
    return -(-rows // 16) * 16


def layout():
    at, places = QROWS, []
    for k0, k1 in KEY_CUTS:
        places.append((at, at + padded(k1 - k0)))
        at += 2 * padded(k1 - k0)
    return places, at


def pack_kernel(place_ref, q_hbm, k_hbm, v_hbm, *refs):
    outs, (q_buf, k_buf, v_buf, sems) = refs[:RING], refs[RING:]
    places, _ = layout()
    order = (1, 3, 2, 0)
    copies = {}
    for d in order:
        group = lax.rem(place_ref[0] + d, RING)
        lanes = pl.ds(pl.multiple_of(group * (RING * PAIR), RING * PAIR), RING * PAIR)
        copies[d] = [
            pltpu.make_async_copy(source.at[:, lanes], target.at[d], sems.at[d, n])
            for n, (source, target) in enumerate(((q_hbm, q_buf), (k_hbm, k_buf), (v_hbm, v_buf)))
        ]
        for copy in copies[d]:
            copy.start()
    for d in order:
        for copy in copies[d]:
            copy.wait()
        out = outs[d]
        for e in range(RING):
            pair = lax.rem(place_ref[1] + e, RING)
            lanes = pl.ds(pl.multiple_of(pair * PAIR, PAIR), PAIR)
            out[e, 0:QROWS] = head_norm(q_buf[d, :, lanes])
            keys = head_norm(k_buf[d, :, lanes])
            for (k0, k1), (kp, vp) in zip(KEY_CUTS, places):
                out[e, kp : kp + k1 - k0] = keys[k0:k1]
                out[e, vp : vp + k1 - k0] = v_buf[d, k0:k1, lanes]
                gap = padded(k1 - k0) - (k1 - k0)
                if gap:
                    out[e, vp - gap : vp] = jnp.zeros((gap, PAIR), jnp.bfloat16)
                    out[e, vp + k1 - k0 : vp + k1 - k0 + gap] = jnp.zeros((gap, PAIR), jnp.bfloat16)


def pack(place, queries, keys, values):
    _, rows = layout()
    vmem = pl.BlockSpec(memory_space=pltpu.VMEM)
    wide = RING * PAIR
    return pl.pallas_call(
        pack_kernel,
        in_specs=[pl.BlockSpec(memory_space=pltpu.SMEM)] + [pl.BlockSpec(memory_space=pl.ANY)] * 3,
        out_specs=[vmem] * RING,
        out_shape=[jax.ShapeDtypeStruct((RING, rows, PAIR), jnp.bfloat16)] * RING,
        scratch_shapes=[
            pltpu.VMEM((RING, QROWS, wide), jnp.bfloat16),
            pltpu.VMEM((RING, KROWS, wide), jnp.bfloat16),
            pltpu.VMEM((RING, KROWS, wide), jnp.bfloat16),
            pltpu.SemaphoreType.DMA((RING, 3)),
        ],
        compiler_params=pltpu.CompilerParams(vmem_limit_bytes=24 * MIB),
        cost_estimate=pl.CostEstimate(flops=2 * 2 * rows * HD * PAIR, bytes_accessed=4 * rows * HD, transcendentals=0),
        name="pack",
    )(place, queries, keys, values)


def first_hop(parts):
    return [parts[0]] + [send(parts[d], True, d) for d in range(1, RING)]


def second_hop(landed, start, stop):
    staged = [jnp.stack([part[e, start:stop] for part in landed]) for e in range(RING)]
    return [staged[0]] + [send(staged[e], False, e) for e in range(1, RING)]


def give_back(blocks):
    landed = [blocks[0]] + [send(blocks[e], False, -e) for e in range(1, RING)]
    staged = [jnp.stack([block[d] for block in landed]) for d in range(RING)]
    return [staged[0]] + [send(staged[d], True, -d) for d in range(1, RING)]


def cuts_of(total, step):
    return [(start, min(step, total - start)) for start in range(0, total, step)]


def attend_kernel(nk, kp, vp, first, last, *refs):
    q_refs, refs = refs[:RING], refs[RING:]
    if first:
        kv_refs = q_refs
    else:
        kv_refs, refs = refs[:RING], refs[RING:]
        acc_in, refs = refs[0], refs[1:]
    if last:
        out_refs, refs = refs[:RING], refs[RING:]
    else:
        acc_out, refs = refs[0], refs[1:]
    q_all, k_all, low_t, high_t = refs
    nr = QROWS
    total = RING * RING * nk
    row = lax.broadcasted_iota(jnp.int32, (PAIR, PAIR), 0)
    col = lax.broadcasted_iota(jnp.int32, (PAIR, PAIR), 1)
    eye = (row == col).astype(jnp.bfloat16)
    for e in range(RING):
        for d in range(RING):
            slot = e * RING + d
            q_all[slot * nr : (slot + 1) * nr] = q_refs[e][d, 0:nr]
            k_all[slot * nk : (slot + 1) * nk] = kv_refs[e][d, kp : kp + nk]
    ones = jnp.ones((VROWS - HEAD_DIM, total), jnp.bfloat16)
    low_t[HEAD_DIM:, :] = ones
    high_t[HEAD_DIM:, :] = ones
    for e in range(RING):
        joined = jnp.concatenate([kv_refs[e][d, vp : vp + nk] for d in range(RING)], axis=0)
        turned = lax.dot_general(eye, joined, NT, preferred_element_type=jnp.float32).astype(jnp.bfloat16)
        low_t[0:HEAD_DIM, e * RING * nk : (e + 1) * RING * nk] = turned[:HEAD_DIM]
        high_t[0:HEAD_DIM, e * RING * nk : (e + 1) * RING * nk] = turned[HEAD_DIM:]
    values_t = (low_t, high_t)
    work = [(h, start, size) for start, size in cuts_of(total, TILE) for h in range(2)]

    @pl.loop(0, RING * RING * nr // BLOCK_Q)
    def _(block):
        q0 = pl.multiple_of(block * BLOCK_Q, BLOCK_Q)
        q = q_all[pl.ds(q0, BLOCK_Q), :]
        lane = lax.broadcasted_iota(jnp.int32, q.shape, 1)
        zero = jnp.zeros_like(q)
        halves = (jnp.where(lane < HEAD_DIM, q, zero), jnp.where(lane < HEAD_DIM, zero, q))
        sums = [jnp.zeros((VROWS, BLOCK_Q), jnp.float32) for _ in range(2)]

        def score(item):
            h, start, size = item
            return lax.dot_general(k_all[start : start + size, :], halves[h], NT, preferred_element_type=jnp.float32)

        ahead = score(work[0])
        for i, (h, start, size) in enumerate(work):
            now = ahead
            if i + 1 < len(work):
                ahead = score(work[i + 1])
            weights = jnp.exp2(now * SCALE).astype(jnp.bfloat16)
            sums[h] = sums[h] + jnp.dot(
                values_t[h][:, start : start + size], weights, preferred_element_type=jnp.float32
            )
        kept = HEAD_DIM + 8
        if not first:
            sums = [sums[h][:kept] + acc_in[h, :, pl.ds(q0, BLOCK_Q)] for h in range(2)]
        if not last:
            for h in range(2):
                acc_out[h, :, pl.ds(q0, BLOCK_Q)] = sums[h][:kept]
        else:
            done = jnp.concatenate([s[:HEAD_DIM] / s[HEAD_DIM : HEAD_DIM + 1] for s in sums], axis=0)
            q_all[pl.ds(q0, BLOCK_Q), :] = done.T.astype(jnp.bfloat16)

    if last:
        for e in range(RING):
            for d in range(RING):
                slot = e * RING + d
                out_refs[e][d] = q_all[slot * nr : (slot + 1) * nr]


def attend(q_parts, kv_parts, acc, nk, kp, vp, last):
    first = acc is None
    nr = QROWS
    nq = RING * RING * nr
    total = RING * RING * nk
    operands = list(q_parts) + ([] if first else list(kv_parts) + [acc])
    vmem = pl.BlockSpec(memory_space=pltpu.VMEM)
    if last:
        out_shape = [jax.ShapeDtypeStruct((RING, nr, PAIR), jnp.bfloat16)] * RING
    else:
        out_shape = [jax.ShapeDtypeStruct((2, HEAD_DIM + 8, nq), jnp.float32)]
    return pl.pallas_call(
        functools.partial(attend_kernel, nk, kp, vp, first, last),
        in_specs=[vmem] * len(operands),
        out_specs=[vmem] * len(out_shape),
        out_shape=out_shape,
        scratch_shapes=[
            pltpu.VMEM((nq, PAIR), jnp.bfloat16),
            pltpu.VMEM((total, PAIR), jnp.bfloat16),
            pltpu.VMEM((VROWS, total), jnp.bfloat16),
            pltpu.VMEM((VROWS, total), jnp.bfloat16),
        ],
        compiler_params=pltpu.CompilerParams(vmem_limit_bytes=32 * MIB),
        cost_estimate=pl.CostEstimate(
            flops=2 * 2 * 4 * nq * total * PAIR, bytes_accessed=2 * MIB, transcendentals=2 * nq * total
        ),
        name="attend",
    )(*operands)


def project_kernel(place_ref, level_ref, *refs):
    parts, refs = refs[:RING], refs[RING:]
    hidden_ref, w_proj_ref, w_final_ref, base_ref, slope_ref, out_ref, drift_ref, joined, gated = refs
    for d in range(RING):
        for e in range(RING):
            pair = lax.rem(place_ref[0] + d, RING) * RING + lax.rem(place_ref[1] + e, RING)
            joined[:, pl.ds(pl.multiple_of(pair * PAIR, PAIR), PAIR)] = parts[d][e]
    squares = jnp.zeros((QROWS, 1), jnp.float32)
    for start, size in cuts_of(D, 512):
        cols = slice(start, start + size)
        projected = jnp.dot(joined[...], w_proj_ref[:, cols], preferred_element_type=jnp.float32)
        gate = base_ref[:, cols] + level_ref[0] * slope_ref[:, cols]
        value = hidden_ref[:, cols].astype(jnp.float32) + gate * projected
        gated[:, cols] = value
        squares = squares + jnp.sum(value * value, axis=1, keepdims=True)
    normed = (gated[...] * lax.rsqrt(squares * (1.0 / D) + 1e-06)).astype(jnp.bfloat16)
    velocity = jnp.dot(normed, w_final_ref[...], preferred_element_type=jnp.float32)
    out_ref[...] = velocity
    half = QROWS // 2
    drift_ref[...] = jnp.concatenate([velocity[:half], velocity[half:]], axis=1) * level_ref[1]


def project(place, level, parts, hidden, w_proj, w_final, base, slope):
    nr = QROWS
    vmem = pl.BlockSpec(memory_space=pltpu.VMEM)
    smem = pl.BlockSpec(memory_space=pltpu.SMEM)
    return pl.pallas_call(
        project_kernel,
        in_specs=[smem, smem] + [vmem] * (RING + 5),
        out_specs=[vmem, vmem],
        out_shape=[
            jax.ShapeDtypeStruct((nr, LAT), jnp.float32),
            jax.ShapeDtypeStruct((nr // 2, 2 * LAT), jnp.float32),
        ],
        scratch_shapes=[pltpu.VMEM((nr, HD), jnp.bfloat16), pltpu.VMEM((nr, D), jnp.float32)],
        compiler_params=pltpu.CompilerParams(vmem_limit_bytes=32 * MIB),
        cost_estimate=pl.CostEstimate(flops=2 * nr * HD * D, bytes_accessed=12 * MIB, transcendentals=0),
        name="project",
    )(place, level, *parts, hidden, w_proj, w_final, base, slope)


def sigma_of(index_val, total_steps):
    frac = 1.0 - index_val.astype(jnp.float32) / total_steps
    return 3.0 * frac / (1.0 + 2.0 * frac)


def running_sum(drift, slots):
    shift = 1
    while shift < slots:
        drift = drift + lax.ppermute(drift.astype(jnp.bfloat16), "tm", [(i, i + shift) for i in range(slots - shift)]).astype(
            jnp.float32
        )
        shift *= 2
    return drift


def per_device(
    queries, keys, values, hidden, w_proj, w_final, gate_base, gate_slope, start_latent, window_steps
):
    slots = lax.axis_size("tm")
    slot = lax.axis_index("tm")
    seat = lax.axis_index("seq")
    x, z = seat // RING, lax.rem(seat, RING)
    even = lax.rem(slot, 2) == 0
    first, second = jnp.where(even, x, z), jnp.where(even, z, x)
    place = jnp.stack([first, second]).astype(jnp.int32)
    sigma_now = sigma_of(window_steps[slot], 2 * slots)
    step_size = sigma_of(window_steps[slot + 1], 2 * slots) - sigma_now
    level = jnp.stack([sigma_now, step_size])

    places, end = layout()
    starts = [0] + [kp for kp, _ in places[1:]] + [end]
    landed = first_hop(pack(place, queries[0], keys[0], values[0]))
    received = [second_hop(landed, start, stop) for start, stop in zip(starts, starts[1:])]
    acc = None
    for number, ((k0, k1), (kp, vp)) in enumerate(zip(KEY_CUTS, places)):
        start = starts[number]
        last = number == len(KEY_CUTS) - 1
        got = attend(received[0], received[number], acc, k1 - k0, kp - start, vp - start, last)
        acc = None if last else got[0]
    velocity, drift = project(
        place, level, give_back(got), hidden[0], w_proj, w_final, gate_base[None], gate_slope[None]
    )
    drift = running_sum(drift, slots)
    half = QROWS // 2
    latents = start_latent + jnp.concatenate([drift[:, :LAT], drift[:, LAT:]], axis=0)
    return (velocity[None], latents[None])


def solution(mesh):
    placed = (
        P("tm", "seq", None),
        P("tm", "seq", None),
        P("tm", "seq", None),
        P("tm", "seq", None),
        P(),
        P(),
        P(),
        P(),
        P("seq", None),
        P(),
    )
    return jax.shard_map(
        per_device,
        mesh=mesh,
        in_specs=placed,
        out_specs=(P("tm", "seq", None), P("tm", "seq", None)),
        check_vma=False,
    )
```

```python
import functools

import jax
import jax.numpy as jnp
from jax import lax
from jax.experimental import pallas as pl
from jax.experimental.pallas import tpu as pltpu
from jax.sharding import PartitionSpec as P

HEADS = 32
HEAD_DIM = 64
HD = 2048
D = 2432
LAT = 64
PAIR = 128
RING = 4
SLOTS = 8
BOTH = ("tm", "seq")
NT = (((1,), (1,)), ((), ()))
SCALE = 0.125 * 1.4426950408889634
KEY_CUTS = ((0, 96), (96, 280))
QROWS = 256
KROWS = 280
TILE = 512
BLOCK_Q = 1024
VROWS = 128
MIB = 2**20


def ring_perm(first, shift):
    pairs = []
    for slot in range(8):
        for place in range(16):
            x, z = divmod(place, RING)
            if (slot % 2 == 0) == first:
                x2, z2 = (x + shift) % RING, z
            else:
                x2, z2 = x, (z + shift) % RING
            pairs.append((slot * 16 + place, slot * 16 + x2 * RING + z2))
    return pairs


def send(value, first, shift):
    return lax.ppermute(value, BOTH, ring_perm(first, shift % RING))


def head_norm(block):
    wide = block.astype(jnp.float32)
    square = wide * wide
    high = square.astype(jnp.bfloat16)
    low = (square - high.astype(jnp.float32)).astype(jnp.bfloat16)
    row = lax.broadcasted_iota(jnp.int32, (PAIR, PAIR), 0)
    col = lax.broadcasted_iota(jnp.int32, (PAIR, PAIR), 1)
    same = ((row < HEAD_DIM) == (col < HEAD_DIM)).astype(jnp.bfloat16)
    total = jnp.dot(high, same, preferred_element_type=jnp.float32)
    total = total + jnp.dot(low, same, preferred_element_type=jnp.float32)
    return (wide * lax.rsqrt(total * (1.0 / HEAD_DIM) + 1e-06)).astype(jnp.bfloat16)


def padded(rows):
    return -(-rows // 16) * 16


def layout():
    at, places = QROWS, []
    for k0, k1 in KEY_CUTS:
        places.append((at, at + padded(k1 - k0)))
        at += 2 * padded(k1 - k0)
    return places, at


def pack_kernel(place_ref, q_hbm, k_hbm, v_hbm, *refs):
    outs, (q_buf, k_buf, v_buf, sems) = refs[:RING], refs[RING:]
    places, _ = layout()
    order = (1, 3, 2, 0)
    copies = {}
    for d in order:
        group = lax.rem(place_ref[0] + d, RING)
        lanes = pl.ds(pl.multiple_of(group * (RING * PAIR), RING * PAIR), RING * PAIR)
        copies[d] = [
            pltpu.make_async_copy(source.at[:, lanes], target.at[d], sems.at[d, n])
            for n, (source, target) in enumerate(((q_hbm, q_buf), (k_hbm, k_buf), (v_hbm, v_buf)))
        ]
        for copy in copies[d]:
            copy.start()
    for d in order:
        for copy in copies[d]:
            copy.wait()
        out = outs[d]
        for e in range(RING):
            pair = lax.rem(place_ref[1] + e, RING)
            lanes = pl.ds(pl.multiple_of(pair * PAIR, PAIR), PAIR)
            out[e, 0:QROWS] = head_norm(q_buf[d, :, lanes])
            keys = head_norm(k_buf[d, :, lanes])
            for (k0, k1), (kp, vp) in zip(KEY_CUTS, places):
                out[e, kp : kp + k1 - k0] = keys[k0:k1]
                out[e, vp : vp + k1 - k0] = v_buf[d, k0:k1, lanes]
                gap = padded(k1 - k0) - (k1 - k0)
                if gap:
                    out[e, vp - gap : vp] = jnp.zeros((gap, PAIR), jnp.bfloat16)
                    out[e, vp + k1 - k0 : vp + k1 - k0 + gap] = jnp.zeros((gap, PAIR), jnp.bfloat16)


def pack(place, queries, keys, values):
    _, rows = layout()
    vmem = pl.BlockSpec(memory_space=pltpu.VMEM)
    wide = RING * PAIR
    return pl.pallas_call(
        pack_kernel,
        in_specs=[pl.BlockSpec(memory_space=pltpu.SMEM)] + [pl.BlockSpec(memory_space=pltpu.HBM)] * 3,
        out_specs=[vmem] * RING,
        out_shape=[jax.ShapeDtypeStruct((RING, rows, PAIR), jnp.bfloat16)] * RING,
        scratch_shapes=[
            pltpu.VMEM((RING, QROWS, wide), jnp.bfloat16),
            pltpu.VMEM((RING, KROWS, wide), jnp.bfloat16),
            pltpu.VMEM((RING, KROWS, wide), jnp.bfloat16),
            pltpu.SemaphoreType.DMA((RING, 3)),
        ],
        compiler_params=pltpu.CompilerParams(vmem_limit_bytes=24 * MIB),
        cost_estimate=pl.CostEstimate(flops=2 * 2 * rows * HD * PAIR, bytes_accessed=4 * rows * HD, transcendentals=0),
        name="pack",
    )(place, queries, keys, values)


def first_hop(parts):
    return [parts[0]] + [send(parts[d], True, d) for d in range(1, RING)]


def second_hop(landed, start, stop):
    staged = [jnp.stack([part[e, start:stop] for part in landed]) for e in range(RING)]
    return [staged[0]] + [send(staged[e], False, e) for e in range(1, RING)]


def cuts_of(total, step):
    return [(start, min(step, total - start)) for start in range(0, total, step)]


def attend_kernel(nk, kp, vp, first, last, place_ref, *refs):
    q_refs, refs = refs[:RING], refs[RING:]
    if first:
        kv_refs = q_refs
    else:
        kv_refs, refs = refs[:RING], refs[RING:]
        acc_in, refs = refs[0], refs[1:]
    if last:
        out_ref, refs = refs[0], refs[1:]
    else:
        acc_out, refs = refs[0], refs[1:]
    q_all, k_all, low_t, high_t = refs
    nr = QROWS
    total = RING * RING * nk
    row = lax.broadcasted_iota(jnp.int32, (PAIR, PAIR), 0)
    col = lax.broadcasted_iota(jnp.int32, (PAIR, PAIR), 1)
    eye = (row == col).astype(jnp.bfloat16)
    for e in range(RING):
        for d in range(RING):
            slot = e * RING + d
            q_all[slot * nr : (slot + 1) * nr] = q_refs[e][d, 0:nr]
            k_all[slot * nk : (slot + 1) * nk] = kv_refs[e][d, kp : kp + nk]
    ones = jnp.ones((VROWS - HEAD_DIM, total), jnp.bfloat16)
    low_t[HEAD_DIM:, :] = ones
    high_t[HEAD_DIM:, :] = ones
    for e in range(RING):
        joined = jnp.concatenate([kv_refs[e][d, vp : vp + nk] for d in range(RING)], axis=0)
        turned = lax.dot_general(eye, joined, NT, preferred_element_type=jnp.float32).astype(jnp.bfloat16)
        low_t[0:HEAD_DIM, e * RING * nk : (e + 1) * RING * nk] = turned[:HEAD_DIM]
        high_t[0:HEAD_DIM, e * RING * nk : (e + 1) * RING * nk] = turned[HEAD_DIM:]
    values_t = (low_t, high_t)
    work = [(h, start, size) for start, size in cuts_of(total, TILE) for h in range(2)]

    @pl.loop(0, RING * RING * nr // BLOCK_Q)
    def _(block):
        q0 = pl.multiple_of(block * BLOCK_Q, BLOCK_Q)
        q = q_all[pl.ds(q0, BLOCK_Q), :]
        lane = lax.broadcasted_iota(jnp.int32, q.shape, 1)
        zero = jnp.zeros_like(q)
        halves = (jnp.where(lane < HEAD_DIM, q, zero), jnp.where(lane < HEAD_DIM, zero, q))
        sums = [jnp.zeros((VROWS, BLOCK_Q), jnp.float32) for _ in range(2)]

        def score(item):
            h, start, size = item
            return lax.dot_general(k_all[start : start + size, :], halves[h], NT, preferred_element_type=jnp.float32)

        ahead = score(work[0])
        for i, (h, start, size) in enumerate(work):
            now = ahead
            if i + 1 < len(work):
                ahead = score(work[i + 1])
            weights = jnp.exp2(now * SCALE).astype(jnp.bfloat16)
            sums[h] = sums[h] + jnp.dot(
                values_t[h][:, start : start + size], weights, preferred_element_type=jnp.float32
            )
        kept = HEAD_DIM + 8
        if not first:
            sums = [sums[h][:kept] + acc_in[h, :, pl.ds(q0, BLOCK_Q)] for h in range(2)]
        if not last:
            for h in range(2):
                acc_out[h, :, pl.ds(q0, BLOCK_Q)] = sums[h][:kept]
        else:
            done = jnp.concatenate([s[:HEAD_DIM] / s[HEAD_DIM : HEAD_DIM + 1] for s in sums], axis=0)
            q_all[pl.ds(q0, BLOCK_Q), :] = done.T.astype(jnp.bfloat16)

    if last:
        for e in range(RING):
            for d in range(RING):
                slot = e * RING + d
                along = lax.rem(place_ref[0] + RING - d, RING)
                across = lax.rem(place_ref[1] + RING - e, RING)
                out_ref[along * place_ref[2] + across * place_ref[3]] = q_all[slot * nr : (slot + 1) * nr]


def attend(place, q_parts, kv_parts, acc, nk, kp, vp, last):
    first = acc is None
    nr = QROWS
    nq = RING * RING * nr
    total = RING * RING * nk
    operands = list(q_parts) + ([] if first else list(kv_parts) + [acc])
    vmem = pl.BlockSpec(memory_space=pltpu.VMEM)
    if last:
        out_shape = [jax.ShapeDtypeStruct((RING * RING, nr, PAIR), jnp.bfloat16)]
    else:
        out_shape = [jax.ShapeDtypeStruct((2, HEAD_DIM + 8, nq), jnp.float32)]
    return pl.pallas_call(
        functools.partial(attend_kernel, nk, kp, vp, first, last),
        in_specs=[pl.BlockSpec(memory_space=pltpu.SMEM)] + [vmem] * len(operands),
        out_specs=[vmem] * len(out_shape),
        out_shape=out_shape,
        scratch_shapes=[
            pltpu.VMEM((nq, PAIR), jnp.bfloat16),
            pltpu.VMEM((total, PAIR), jnp.bfloat16),
            pltpu.VMEM((VROWS, total), jnp.bfloat16),
            pltpu.VMEM((VROWS, total), jnp.bfloat16),
        ],
        compiler_params=pltpu.CompilerParams(vmem_limit_bytes=20 * MIB),
        cost_estimate=pl.CostEstimate(
            flops=2 * 2 * 4 * nq * total * PAIR, bytes_accessed=2 * MIB, transcendentals=2 * nq * total
        ),
        name="attend",
    )(place, *operands)


def project_kernel(place_ref, level_ref, got_ref, hidden_ref, w_proj_ref, w_final_ref, base_ref, slope_ref, *refs):
    velocity_ref, drift_ref, later_ref, joined, gated = refs
    for j in range(RING * RING):
        hi, lo = divmod(j, RING)
        pair = hi * place_ref[2] + lo * place_ref[3]
        joined[:, pl.ds(pl.multiple_of(pair * PAIR, PAIR), PAIR)] = got_ref[j]
    squares = jnp.zeros((QROWS, 1), jnp.float32)
    for start, size in cuts_of(D, 512):
        cols = slice(start, start + size)
        projected = jnp.dot(joined[...], w_proj_ref[:, cols], preferred_element_type=jnp.float32)
        gate = base_ref[:, cols] + level_ref[0] * slope_ref[:, cols]
        value = hidden_ref[:, cols].astype(jnp.float32) + gate * projected
        gated[:, cols] = value
        squares = squares + jnp.sum(value * value, axis=1, keepdims=True)
    normed = (gated[...] * lax.rsqrt(squares * (1.0 / D) + 1e-06)).astype(jnp.bfloat16)
    velocity = lax.dot_general(w_final_ref[...], normed, NT, preferred_element_type=jnp.float32)
    velocity_ref[...] = velocity
    drift = velocity * level_ref[1]
    drift_ref[...] = drift
    low = drift.astype(jnp.bfloat16)
    for k in range(SLOTS):
        later_ref[k] = jnp.where(place_ref[4] < k, low, jnp.zeros_like(low))


def project(place, level, got, hidden, w_proj, w_final, base, slope):
    vmem = pl.BlockSpec(memory_space=pltpu.VMEM)
    smem = pl.BlockSpec(memory_space=pltpu.SMEM)
    return pl.pallas_call(
        project_kernel,
        in_specs=[smem, smem] + [vmem] * 6,
        out_specs=[vmem] * 3,
        out_shape=[
            jax.ShapeDtypeStruct((LAT, QROWS), jnp.float32),
            jax.ShapeDtypeStruct((LAT, QROWS), jnp.float32),
            jax.ShapeDtypeStruct((SLOTS, LAT, QROWS), jnp.bfloat16),
        ],
        scratch_shapes=[pltpu.VMEM((QROWS, HD), jnp.bfloat16), pltpu.VMEM((QROWS, D), jnp.float32)],
        compiler_params=pltpu.CompilerParams(vmem_limit_bytes=16 * MIB),
        cost_estimate=pl.CostEstimate(flops=2 * QROWS * HD * D, bytes_accessed=12 * MIB, transcendentals=0),
        name="project",
    )(place, level, got, hidden, w_proj, w_final, base, slope)


def sigma_of(index_val, total_steps):
    frac = 1.0 - index_val.astype(jnp.float32) / total_steps
    return 3.0 * frac / (1.0 + 2.0 * frac)


def per_device(
    queries, keys, values, hidden, w_proj, w_final, gate_base, gate_slope, start_latent, window_steps
):
    slots = lax.axis_size("tm")
    slot = lax.axis_index("tm")
    seat = lax.axis_index("seq")
    x, z = seat // RING, lax.rem(seat, RING)
    even = lax.rem(slot, 2) == 0
    first, second = jnp.where(even, x, z), jnp.where(even, z, x)
    place = jnp.stack([first, second, jnp.where(even, RING, 1), jnp.where(even, 1, RING), slot]).astype(jnp.int32)
    sigma_now = sigma_of(window_steps[slot], 2 * slots)
    step_size = sigma_of(window_steps[slot + 1], 2 * slots) - sigma_now
    level = jnp.stack([sigma_now, step_size])

    places, end = layout()
    starts = [0] + [kp for kp, _ in places[1:]] + [end]
    landed = first_hop(pack(place, queries[0], keys[0], values[0]))
    received = [second_hop(landed, start, stop) for start, stop in zip(starts, starts[1:])]
    acc = None
    for number, ((k0, k1), (kp, vp)) in enumerate(zip(KEY_CUTS, places)):
        start = starts[number]
        last = number == len(KEY_CUTS) - 1
        got = attend(place, received[0], received[number], acc, k1 - k0, kp - start, vp - start, last)
        acc = None if last else got[0]
    got = lax.all_to_all(got[0], "seq", 0, 0, tiled=True)
    velocity, drift, later = project(
        place, level, got, hidden[0], w_proj, w_final.T, gate_base[None], gate_slope[None]
    )
    earlier = lax.all_to_all(later, "tm", 0, 0, tiled=True).astype(jnp.float32)
    latents = start_latent.T + drift + jnp.sum(earlier, axis=0)
    return (velocity.T[None], latents.T[None])


def solution(mesh):
    placed = (
        P("tm", "seq", None),
        P("tm", "seq", None),
        P("tm", "seq", None),
        P("tm", "seq", None),
        P(),
        P(),
        P(),
        P(),
        P("seq", None),
        P(),
    )
    return jax.shard_map(
        per_device,
        mesh=mesh,
        in_specs=placed,
        out_specs=(P("tm", "seq", None), P("tm", "seq", None)),
        check_vma=False,
    )
```

```python
import functools

import jax
import jax.numpy as jnp
from jax import lax
from jax.experimental import pallas as pl
from jax.experimental.pallas import tpu as pltpu
from jax.sharding import PartitionSpec as P

HEADS = 32
HEAD_DIM = 64
HD = 2048
D = 2432
LAT = 64
PAIR = 128
RING = 4
SLOTS = 8
BOTH = ("tm", "seq")
NT = (((1,), (1,)), ((), ()))
SCALE = 0.125 * 1.4426950408889634
KEY_CUTS = ((0, 96), (96, 280))
QROWS = 256
KROWS = 280
TILE = 512
BLOCK_Q = 1024
VROWS = 128
MIB = 2**20


def ring_perm(first, shift):
    pairs = []
    for slot in range(8):
        for place in range(16):
            x, z = divmod(place, RING)
            if (slot % 2 == 0) == first:
                x2, z2 = (x + shift) % RING, z
            else:
                x2, z2 = x, (z + shift) % RING
            pairs.append((slot * 16 + place, slot * 16 + x2 * RING + z2))
    return pairs


def send(value, first, shift):
    return lax.ppermute(value, BOTH, ring_perm(first, shift % RING))


def head_norm(block):
    wide = block.astype(jnp.float32)
    square = wide * wide
    high = square.astype(jnp.bfloat16)
    low = (square - high.astype(jnp.float32)).astype(jnp.bfloat16)
    row = lax.broadcasted_iota(jnp.int32, (PAIR, PAIR), 0)
    col = lax.broadcasted_iota(jnp.int32, (PAIR, PAIR), 1)
    same = ((row < HEAD_DIM) == (col < HEAD_DIM)).astype(jnp.bfloat16)
    total = jnp.dot(high, same, preferred_element_type=jnp.float32)
    total = total + jnp.dot(low, same, preferred_element_type=jnp.float32)
    return (wide * lax.rsqrt(total * (1.0 / HEAD_DIM) + 1e-06)).astype(jnp.bfloat16)


def padded(rows):
    return -(-rows // 16) * 16


def layout():
    at, places = QROWS, []
    for k0, k1 in KEY_CUTS:
        places.append((at, at + padded(k1 - k0)))
        at += 2 * padded(k1 - k0)
    return places, at


def pack_kernel(place_ref, q_hbm, k_hbm, v_hbm, *refs):
    outs, (q_buf, k_buf, v_buf, sems) = refs[:RING], refs[RING:]
    places, _ = layout()
    order = (1, 3, 2, 0)
    copies = {}
    for d in order:
        group = lax.rem(place_ref[0] + d, RING)
        lanes = pl.ds(pl.multiple_of(group * (RING * PAIR), RING * PAIR), RING * PAIR)
        copies[d] = [
            pltpu.make_async_copy(source.at[:, lanes], target.at[d], sems.at[d, n])
            for n, (source, target) in enumerate(((q_hbm, q_buf), (k_hbm, k_buf), (v_hbm, v_buf)))
        ]
        for copy in copies[d]:
            copy.start()
    for d in order:
        for copy in copies[d]:
            copy.wait()
        out = outs[d]
        for e in range(RING):
            pair = lax.rem(place_ref[1] + e, RING)
            lanes = pl.ds(pl.multiple_of(pair * PAIR, PAIR), PAIR)
            out[e, 0:QROWS] = head_norm(q_buf[d, :, lanes])
            keys = head_norm(k_buf[d, :, lanes])
            for (k0, k1), (kp, vp) in zip(KEY_CUTS, places):
                out[e, kp : kp + k1 - k0] = keys[k0:k1]
                out[e, vp : vp + k1 - k0] = v_buf[d, k0:k1, lanes]
                gap = padded(k1 - k0) - (k1 - k0)
                if gap:
                    out[e, vp - gap : vp] = jnp.zeros((gap, PAIR), jnp.bfloat16)
                    out[e, vp + k1 - k0 : vp + k1 - k0 + gap] = jnp.zeros((gap, PAIR), jnp.bfloat16)


def pack(place, queries, keys, values):
    _, rows = layout()
    vmem = pl.BlockSpec(memory_space=pltpu.VMEM)
    wide = RING * PAIR
    return pl.pallas_call(
        pack_kernel,
        in_specs=[pl.BlockSpec(memory_space=pltpu.SMEM)] + [pl.BlockSpec(memory_space=pltpu.HBM)] * 3,
        out_specs=[vmem] * RING,
        out_shape=[jax.ShapeDtypeStruct((RING, rows, PAIR), jnp.bfloat16)] * RING,
        scratch_shapes=[
            pltpu.VMEM((RING, QROWS, wide), jnp.bfloat16),
            pltpu.VMEM((RING, KROWS, wide), jnp.bfloat16),
            pltpu.VMEM((RING, KROWS, wide), jnp.bfloat16),
            pltpu.SemaphoreType.DMA((RING, 3)),
        ],
        compiler_params=pltpu.CompilerParams(vmem_limit_bytes=59 * MIB),
        cost_estimate=pl.CostEstimate(flops=2 * 2 * rows * HD * PAIR, bytes_accessed=4 * rows * HD, transcendentals=0),
        name="pack",
    )(place, queries, keys, values)


def first_hop(parts):
    return [parts[0]] + [send(parts[d], True, d) for d in range(1, RING)]


def second_hop(landed, start, stop):
    staged = [jnp.stack([part[e, start:stop] for part in landed]) for e in range(RING)]
    return [staged[0]] + [send(staged[e], False, e) for e in range(1, RING)]


def cuts_of(total, step):
    return [(start, min(step, total - start)) for start in range(0, total, step)]


def attend_kernel(nk, kp, vp, first, last, place_ref, *refs):
    q_refs, refs = refs[:RING], refs[RING:]
    if first:
        kv_refs = q_refs
    else:
        kv_refs, refs = refs[:RING], refs[RING:]
        acc_in, refs = refs[0], refs[1:]
    if last:
        out_ref, refs = refs[0], refs[1:]
    else:
        acc_out, refs = refs[0], refs[1:]
    q_all, k_all, low_t, high_t = refs
    nr = QROWS
    total = RING * RING * nk
    row = lax.broadcasted_iota(jnp.int32, (PAIR, PAIR), 0)
    col = lax.broadcasted_iota(jnp.int32, (PAIR, PAIR), 1)
    eye = (row == col).astype(jnp.bfloat16)
    for e in range(RING):
        for d in range(RING):
            slot = e * RING + d
            q_all[slot * nr : (slot + 1) * nr] = q_refs[e][d, 0:nr]
            k_all[slot * nk : (slot + 1) * nk] = kv_refs[e][d, kp : kp + nk]
    ones = jnp.ones((VROWS - HEAD_DIM, total), jnp.bfloat16)
    low_t[HEAD_DIM:, :] = ones
    high_t[HEAD_DIM:, :] = ones
    for e in range(RING):
        joined = jnp.concatenate([kv_refs[e][d, vp : vp + nk] for d in range(RING)], axis=0)
        turned = lax.dot_general(eye, joined, NT, preferred_element_type=jnp.float32).astype(jnp.bfloat16)
        low_t[0:HEAD_DIM, e * RING * nk : (e + 1) * RING * nk] = turned[:HEAD_DIM]
        high_t[0:HEAD_DIM, e * RING * nk : (e + 1) * RING * nk] = turned[HEAD_DIM:]
    values_t = (low_t, high_t)
    work = [(h, start, size) for start, size in cuts_of(total, TILE) for h in range(2)]

    @pl.loop(0, RING * RING * nr // BLOCK_Q)
    def _(block):
        q0 = pl.multiple_of(block * BLOCK_Q, BLOCK_Q)
        q = q_all[pl.ds(q0, BLOCK_Q), :]
        lane = lax.broadcasted_iota(jnp.int32, q.shape, 1)
        zero = jnp.zeros_like(q)
        halves = (jnp.where(lane < HEAD_DIM, q, zero), jnp.where(lane < HEAD_DIM, zero, q))
        sums = [jnp.zeros((VROWS, BLOCK_Q), jnp.float32) for _ in range(2)]

        def score(item):
            h, start, size = item
            return lax.dot_general(k_all[start : start + size, :], halves[h], NT, preferred_element_type=jnp.float32)

        ahead = score(work[0])
        for i, (h, start, size) in enumerate(work):
            now = ahead
            if i + 1 < len(work):
                ahead = score(work[i + 1])
            weights = jnp.exp2(now * SCALE).astype(jnp.bfloat16)
            sums[h] = sums[h] + jnp.dot(
                values_t[h][:, start : start + size], weights, preferred_element_type=jnp.float32
            )
        kept = HEAD_DIM + 8
        if not first:
            sums = [sums[h][:kept] + acc_in[h, :, pl.ds(q0, BLOCK_Q)] for h in range(2)]
        if not last:
            for h in range(2):
                acc_out[h, :, pl.ds(q0, BLOCK_Q)] = sums[h][:kept]
        else:
            done = jnp.concatenate([s[:HEAD_DIM] / s[HEAD_DIM : HEAD_DIM + 1] for s in sums], axis=0)
            q_all[pl.ds(q0, BLOCK_Q), :] = done.T.astype(jnp.bfloat16)

    if last:
        for e in range(RING):
            for d in range(RING):
                slot = e * RING + d
                along = lax.rem(place_ref[0] + RING - d, RING)
                across = lax.rem(place_ref[1] + RING - e, RING)
                out_ref[along * place_ref[2] + across * place_ref[3]] = q_all[slot * nr : (slot + 1) * nr]


def attend(place, q_parts, kv_parts, acc, nk, kp, vp, last):
    first = acc is None
    nr = QROWS
    nq = RING * RING * nr
    total = RING * RING * nk
    operands = list(q_parts) + ([] if first else list(kv_parts) + [acc])
    vmem = pl.BlockSpec(memory_space=pltpu.VMEM)
    if last:
        out_shape = [jax.ShapeDtypeStruct((RING * RING, nr, PAIR), jnp.bfloat16)]
    else:
        out_shape = [jax.ShapeDtypeStruct((2, HEAD_DIM + 8, nq), jnp.float32)]
    return pl.pallas_call(
        functools.partial(attend_kernel, nk, kp, vp, first, last),
        in_specs=[pl.BlockSpec(memory_space=pltpu.SMEM)] + [vmem] * len(operands),
        out_specs=[vmem] * len(out_shape),
        out_shape=out_shape,
        scratch_shapes=[
            pltpu.VMEM((nq, PAIR), jnp.bfloat16),
            pltpu.VMEM((total, PAIR), jnp.bfloat16),
            pltpu.VMEM((VROWS, total), jnp.bfloat16),
            pltpu.VMEM((VROWS, total), jnp.bfloat16),
        ],
        compiler_params=pltpu.CompilerParams(vmem_limit_bytes=32 * MIB),
        cost_estimate=pl.CostEstimate(
            flops=2 * 2 * 4 * nq * total * PAIR, bytes_accessed=2 * MIB, transcendentals=2 * nq * total
        ),
        name="attend",
    )(place, *operands)


def project_kernel(place_ref, level_ref, got_ref, hidden_ref, w_proj_ref, w_final_ref, base_ref, slope_ref, *refs):
    velocity_ref, drift_ref, later_ref, joined, gated = refs
    for j in range(RING * RING):
        hi, lo = divmod(j, RING)
        pair = hi * place_ref[2] + lo * place_ref[3]
        joined[:, pl.ds(pl.multiple_of(pair * PAIR, PAIR), PAIR)] = got_ref[j]
    squares = jnp.zeros((QROWS, 1), jnp.float32)
    for start, size in cuts_of(D, 512):
        cols = slice(start, start + size)
        projected = jnp.dot(joined[...], w_proj_ref[:, cols], preferred_element_type=jnp.float32)
        gate = base_ref[:, cols] + level_ref[0] * slope_ref[:, cols]
        value = hidden_ref[:, cols].astype(jnp.float32) + gate * projected
        gated[:, cols] = value
        squares = squares + jnp.sum(value * value, axis=1, keepdims=True)
    normed = (gated[...] * lax.rsqrt(squares * (1.0 / D) + 1e-06)).astype(jnp.bfloat16)
    velocity = lax.dot_general(w_final_ref[...], normed, NT, preferred_element_type=jnp.float32)
    velocity_ref[...] = velocity
    drift = velocity * level_ref[1]
    drift_ref[...] = drift
    low = drift.astype(jnp.bfloat16)
    for k in range(SLOTS):
        later_ref[k] = jnp.where(place_ref[4] < k, low, jnp.zeros_like(low))


def project(place, level, got, hidden, w_proj, w_final, base, slope):
    vmem = pl.BlockSpec(memory_space=pltpu.VMEM)
    smem = pl.BlockSpec(memory_space=pltpu.SMEM)
    return pl.pallas_call(
        project_kernel,
        in_specs=[smem, smem] + [vmem] * 6,
        out_specs=[vmem] * 3,
        out_shape=[
            jax.ShapeDtypeStruct((LAT, QROWS), jnp.float32),
            jax.ShapeDtypeStruct((LAT, QROWS), jnp.float32),
            jax.ShapeDtypeStruct((SLOTS, LAT, QROWS), jnp.bfloat16),
        ],
        scratch_shapes=[pltpu.VMEM((QROWS, HD), jnp.bfloat16), pltpu.VMEM((QROWS, D), jnp.float32)],
        compiler_params=pltpu.CompilerParams(vmem_limit_bytes=16 * MIB),
        cost_estimate=pl.CostEstimate(flops=2 * QROWS * HD * D, bytes_accessed=12 * MIB, transcendentals=0),
        name="project",
    )(place, level, got, hidden, w_proj, w_final, base, slope)


def sigma_of(index_val, total_steps):
    frac = 1.0 - index_val.astype(jnp.float32) / total_steps
    return 3.0 * frac / (1.0 + 2.0 * frac)


def per_device(
    queries, keys, values, hidden, w_proj, w_final, gate_base, gate_slope, start_latent, window_steps
):
    slots = lax.axis_size("tm")
    slot = lax.axis_index("tm")
    seat = lax.axis_index("seq")
    x, z = seat // RING, lax.rem(seat, RING)
    even = lax.rem(slot, 2) == 0
    first, second = jnp.where(even, x, z), jnp.where(even, z, x)
    place = jnp.stack([first, second, jnp.where(even, RING, 1), jnp.where(even, 1, RING), slot]).astype(jnp.int32)
    sigma_now = sigma_of(window_steps[slot], 2 * slots)
    step_size = sigma_of(window_steps[slot + 1], 2 * slots) - sigma_now
    level = jnp.stack([sigma_now, step_size])

    places, end = layout()
    starts = [0] + [kp for kp, _ in places[1:]] + [end]
    landed = first_hop(pack(place, queries[0], keys[0], values[0]))
    received = [second_hop(landed, start, stop) for start, stop in zip(starts, starts[1:])]
    acc = None
    for number, ((k0, k1), (kp, vp)) in enumerate(zip(KEY_CUTS, places)):
        start = starts[number]
        last = number == len(KEY_CUTS) - 1
        got = attend(place, received[0], received[number], acc, k1 - k0, kp - start, vp - start, last)
        acc = None if last else got[0]
    got, *operands = lax.optimization_barrier(
        (got[0], level, hidden[0], w_proj, w_final.T, gate_base[None], gate_slope[None])
    )
    got = lax.all_to_all(got, "seq", 0, 0, tiled=True)
    velocity, drift, later = project(place, operands[0], got, *operands[1:])
    earlier = lax.all_to_all(later, "tm", 0, 0, tiled=True).astype(jnp.float32)
    latents = start_latent.T + drift + jnp.sum(earlier, axis=0)
    return (velocity.T[None], latents.T[None])


def solution(mesh):
    placed = (
        P("tm", "seq", None),
        P("tm", "seq", None),
        P("tm", "seq", None),
        P("tm", "seq", None),
        P(),
        P(),
        P(),
        P(),
        P("seq", None),
        P(),
    )
    return jax.shard_map(
        per_device,
        mesh=mesh,
        in_specs=placed,
        out_specs=(P("tm", "seq", None), P("tm", "seq", None)),
        check_vma=False,
    )
```

```python
import functools

import jax
import jax.numpy as jnp
from jax import lax
from jax.experimental import pallas as pl
from jax.experimental.pallas import tpu as pltpu
from jax.sharding import PartitionSpec as P

HEADS = 32
HEAD_DIM = 64
HD = 2048
D = 2432
LAT = 64
PAIR = 128
RING = 4
SLOTS = 8
BOTH = ("tm", "seq")
NT = (((1,), (1,)), ((), ()))
SCALE = 0.125 * 1.4426950408889634
KEY_CUTS = ((0, 96), (96, 280))
QROWS = 256
KROWS = 280
TILE = 512
BLOCK_Q = 2048
VROWS = 128
MIB = 2**20


def ring_perm(first, shift):
    pairs = []
    for slot in range(8):
        for place in range(16):
            x, z = divmod(place, RING)
            if (slot % 2 == 0) == first:
                x2, z2 = (x + shift) % RING, z
            else:
                x2, z2 = x, (z + shift) % RING
            pairs.append((slot * 16 + place, slot * 16 + x2 * RING + z2))
    return pairs


def send(value, first, shift):
    return lax.ppermute(value, BOTH, ring_perm(first, shift % RING))


def head_norm(block):
    wide = block.astype(jnp.float32)
    square = wide * wide
    high = square.astype(jnp.bfloat16)
    low = (square - high.astype(jnp.float32)).astype(jnp.bfloat16)
    row = lax.broadcasted_iota(jnp.int32, (PAIR, PAIR), 0)
    col = lax.broadcasted_iota(jnp.int32, (PAIR, PAIR), 1)
    same = ((row < HEAD_DIM) == (col < HEAD_DIM)).astype(jnp.bfloat16)
    total = jnp.dot(high, same, preferred_element_type=jnp.float32)
    total = total + jnp.dot(low, same, preferred_element_type=jnp.float32)
    return (wide * lax.rsqrt(total * (1.0 / HEAD_DIM) + 1e-06)).astype(jnp.bfloat16)


def padded(rows):
    return -(-rows // 16) * 16


def layout():
    at, places = QROWS, []
    for k0, k1 in KEY_CUTS:
        places.append((at, at + padded(k1 - k0)))
        at += 2 * padded(k1 - k0)
    return places, at


def pack_kernel(shifts, place_ref, q_hbm, k_hbm, v_hbm, *refs):
    outs, (q_buf, k_buf, v_buf, sems) = refs[: len(shifts)], refs[len(shifts) :]
    places, _ = layout()
    copies = []
    for i, d in enumerate(shifts):
        group = lax.rem(place_ref[0] + d, RING)
        lanes = pl.ds(pl.multiple_of(group * (RING * PAIR), RING * PAIR), RING * PAIR)
        copies.append(
            [
                pltpu.make_async_copy(source.at[:, lanes], target.at[i], sems.at[i, n])
                for n, (source, target) in enumerate(((q_hbm, q_buf), (k_hbm, k_buf), (v_hbm, v_buf)))
            ]
        )
        for copy in copies[i]:
            copy.start()
    for i in range(len(shifts)):
        for copy in copies[i]:
            copy.wait()
        out = outs[i]
        for e in range(RING):
            pair = lax.rem(place_ref[1] + e, RING)
            lanes = pl.ds(pl.multiple_of(pair * PAIR, PAIR), PAIR)
            out[e, 0:QROWS] = head_norm(q_buf[i, :, lanes])
            keys = head_norm(k_buf[i, :, lanes])
            for (k0, k1), (kp, vp) in zip(KEY_CUTS, places):
                out[e, kp : kp + k1 - k0] = keys[k0:k1]
                out[e, vp : vp + k1 - k0] = v_buf[i, k0:k1, lanes]
                gap = padded(k1 - k0) - (k1 - k0)
                if gap:
                    out[e, vp - gap : vp] = jnp.zeros((gap, PAIR), jnp.bfloat16)
                    out[e, vp + k1 - k0 : vp + k1 - k0 + gap] = jnp.zeros((gap, PAIR), jnp.bfloat16)


def pack(place, queries, keys, values, shifts):
    _, rows = layout()
    vmem = pl.BlockSpec(memory_space=pltpu.VMEM)
    wide = RING * PAIR
    count = len(shifts)
    return pl.pallas_call(
        functools.partial(pack_kernel, shifts),
        in_specs=[pl.BlockSpec(memory_space=pltpu.SMEM)] + [pl.BlockSpec(memory_space=pltpu.HBM)] * 3,
        out_specs=[vmem] * count,
        out_shape=[jax.ShapeDtypeStruct((RING, rows, PAIR), jnp.bfloat16)] * count,
        scratch_shapes=[
            pltpu.VMEM((count, QROWS, wide), jnp.bfloat16),
            pltpu.VMEM((count, KROWS, wide), jnp.bfloat16),
            pltpu.VMEM((count, KROWS, wide), jnp.bfloat16),
            pltpu.SemaphoreType.DMA((count, 3)),
        ],
        compiler_params=pltpu.CompilerParams(vmem_limit_bytes=59 * MIB),
        cost_estimate=pl.CostEstimate(
            flops=count * rows * HD * PAIR, bytes_accessed=count * rows * HD, transcendentals=0
        ),
        name="pack",
    )(place, queries, keys, values)


def first_hop(place, queries, keys, values):
    up, down, across, own = pack(place, queries, keys, values, (1, 3, 2, 0))
    return [own, send(up, True, 1), send(across, True, 2), send(down, True, 3)]


def second_hop(landed, start, stop):
    staged = [jnp.stack([part[e, start:stop] for part in landed]) for e in range(RING)]
    return [staged[0]] + [send(staged[e], False, e) for e in range(1, RING)]


def cuts_of(total, step):
    return [(start, min(step, total - start)) for start in range(0, total, step)]


def attend_kernel(nk, kp, vp, first, last, place_ref, *refs):
    q_refs, refs = refs[:RING], refs[RING:]
    if first:
        kv_refs = q_refs
    else:
        kv_refs, refs = refs[:RING], refs[RING:]
        acc_in, refs = refs[0], refs[1:]
    if last:
        out_ref, refs = refs[0], refs[1:]
    else:
        acc_out, refs = refs[0], refs[1:]
    q_all, k_all, low_t, high_t = refs
    nr = QROWS
    total = RING * RING * nk
    row = lax.broadcasted_iota(jnp.int32, (PAIR, PAIR), 0)
    col = lax.broadcasted_iota(jnp.int32, (PAIR, PAIR), 1)
    eye = (row == col).astype(jnp.bfloat16)
    for e in range(RING):
        for d in range(RING):
            slot = e * RING + d
            q_all[slot * nr : (slot + 1) * nr] = q_refs[e][d, 0:nr]
            k_all[slot * nk : (slot + 1) * nk] = kv_refs[e][d, kp : kp + nk]
    ones = jnp.ones((VROWS - HEAD_DIM, total), jnp.bfloat16)
    low_t[HEAD_DIM:, :] = ones
    high_t[HEAD_DIM:, :] = ones
    for e in range(RING):
        joined = jnp.concatenate([kv_refs[e][d, vp : vp + nk] for d in range(RING)], axis=0)
        turned = lax.dot_general(eye, joined, NT, preferred_element_type=jnp.float32).astype(jnp.bfloat16)
        low_t[0:HEAD_DIM, e * RING * nk : (e + 1) * RING * nk] = turned[:HEAD_DIM]
        high_t[0:HEAD_DIM, e * RING * nk : (e + 1) * RING * nk] = turned[HEAD_DIM:]
    values_t = (low_t, high_t)
    work = [(h, start, size) for start, size in cuts_of(total, TILE) for h in range(2)]

    @pl.loop(0, RING * RING * nr // BLOCK_Q)
    def _(block):
        q0 = pl.multiple_of(block * BLOCK_Q, BLOCK_Q)
        q = q_all[pl.ds(q0, BLOCK_Q), :]
        lane = lax.broadcasted_iota(jnp.int32, q.shape, 1)
        zero = jnp.zeros_like(q)
        halves = (jnp.where(lane < HEAD_DIM, q, zero), jnp.where(lane < HEAD_DIM, zero, q))
        sums = [jnp.zeros((VROWS, BLOCK_Q), jnp.float32) for _ in range(2)]

        def score(item):
            h, start, size = item
            return lax.dot_general(k_all[start : start + size, :], halves[h], NT, preferred_element_type=jnp.float32)

        ahead = score(work[0])
        for i, (h, start, size) in enumerate(work):
            now = ahead
            if i + 1 < len(work):
                ahead = score(work[i + 1])
            weights = jnp.exp2(now * SCALE).astype(jnp.bfloat16)
            sums[h] = sums[h] + jnp.dot(
                values_t[h][:, start : start + size], weights, preferred_element_type=jnp.float32
            )
        kept = HEAD_DIM + 8
        if not first:
            sums = [sums[h][:kept] + acc_in[h, :, pl.ds(q0, BLOCK_Q)] for h in range(2)]
        if not last:
            for h in range(2):
                acc_out[h, :, pl.ds(q0, BLOCK_Q)] = sums[h][:kept]
        else:
            done = jnp.concatenate([s[:HEAD_DIM] / s[HEAD_DIM : HEAD_DIM + 1] for s in sums], axis=0)
            q_all[pl.ds(q0, BLOCK_Q), :] = done.T.astype(jnp.bfloat16)

    if last:
        for e in range(RING):
            for d in range(RING):
                slot = e * RING + d
                along = lax.rem(place_ref[0] + RING - d, RING)
                across = lax.rem(place_ref[1] + RING - e, RING)
                out_ref[along * place_ref[2] + across * place_ref[3]] = q_all[slot * nr : (slot + 1) * nr]


def attend(place, q_parts, kv_parts, acc, nk, kp, vp, last):
    first = acc is None
    nr = QROWS
    nq = RING * RING * nr
    total = RING * RING * nk
    operands = list(q_parts) + ([] if first else list(kv_parts) + [acc])
    vmem = pl.BlockSpec(memory_space=pltpu.VMEM)
    if last:
        out_shape = [jax.ShapeDtypeStruct((RING * RING, nr, PAIR), jnp.bfloat16)]
    else:
        out_shape = [jax.ShapeDtypeStruct((2, HEAD_DIM + 8, nq), jnp.float32)]
    return pl.pallas_call(
        functools.partial(attend_kernel, nk, kp, vp, first, last),
        in_specs=[pl.BlockSpec(memory_space=pltpu.SMEM)] + [vmem] * len(operands),
        out_specs=[vmem] * len(out_shape),
        out_shape=out_shape,
        scratch_shapes=[
            pltpu.VMEM((nq, PAIR), jnp.bfloat16),
            pltpu.VMEM((total, PAIR), jnp.bfloat16),
            pltpu.VMEM((VROWS, total), jnp.bfloat16),
            pltpu.VMEM((VROWS, total), jnp.bfloat16),
        ],
        compiler_params=pltpu.CompilerParams(vmem_limit_bytes=32 * MIB),
        cost_estimate=pl.CostEstimate(
            flops=2 * 2 * 4 * nq * total * PAIR, bytes_accessed=2 * MIB, transcendentals=2 * nq * total
        ),
        name="attend",
    )(place, *operands)


def project_kernel(place_ref, level_ref, got_ref, hidden_ref, w_proj_ref, w_final_ref, base_ref, slope_ref, *refs):
    velocity_ref, drift_ref, joined = refs
    for j in range(RING * RING):
        hi, lo = divmod(j, RING)
        pair = hi * place_ref[2] + lo * place_ref[3]
        joined[:, pl.ds(pl.multiple_of(pair * PAIR, PAIR), PAIR)] = got_ref[j]
    squares = jnp.zeros((QROWS, 1), jnp.float32)
    product = jnp.zeros((LAT, QROWS), jnp.float32)
    for start, size in cuts_of(D, 512):
        cols = slice(start, start + size)
        projected = jnp.dot(joined[...], w_proj_ref[:, cols], preferred_element_type=jnp.float32)
        gate = base_ref[:, cols] + level_ref[0] * slope_ref[:, cols]
        value = hidden_ref[:, cols].astype(jnp.float32) + gate * projected
        product = product + lax.dot_general(
            w_final_ref[:, cols], value.astype(jnp.bfloat16), NT, preferred_element_type=jnp.float32
        )
        squares = squares + jnp.sum(value * value, axis=1, keepdims=True)
    along = jnp.broadcast_to(squares, (QROWS, PAIR)).T[0:1]
    velocity = product * lax.rsqrt(along * (1.0 / D) + 1e-06)
    velocity_ref[...] = velocity
    drift = velocity * level_ref[1]
    drift_ref[...] = drift


def project(place, level, got, hidden, w_proj, w_final, base, slope):
    vmem = pl.BlockSpec(memory_space=pltpu.VMEM)
    smem = pl.BlockSpec(memory_space=pltpu.SMEM)
    return pl.pallas_call(
        project_kernel,
        in_specs=[smem, smem] + [vmem] * 6,
        out_specs=[vmem] * 2,
        out_shape=[
            jax.ShapeDtypeStruct((LAT, QROWS), jnp.float32),
            jax.ShapeDtypeStruct((LAT, QROWS), jnp.float32),
        ],
        scratch_shapes=[pltpu.VMEM((QROWS, HD), jnp.bfloat16)],
        compiler_params=pltpu.CompilerParams(vmem_limit_bytes=16 * MIB),
        cost_estimate=pl.CostEstimate(flops=2 * QROWS * HD * D, bytes_accessed=12 * MIB, transcendentals=0),
        name="project",
    )(place, level, got, hidden, w_proj, w_final, base, slope)


def sigma_of(index_val, total_steps):
    frac = 1.0 - index_val.astype(jnp.float32) / total_steps
    return 3.0 * frac / (1.0 + 2.0 * frac)


def per_device(
    queries, keys, values, hidden, w_proj, w_final, gate_base, gate_slope, start_latent, window_steps
):
    slots = lax.axis_size("tm")
    slot = lax.axis_index("tm")
    seat = lax.axis_index("seq")
    x, z = seat // RING, lax.rem(seat, RING)
    even = lax.rem(slot, 2) == 0
    first, second = jnp.where(even, x, z), jnp.where(even, z, x)
    place = jnp.stack([first, second, jnp.where(even, RING, 1), jnp.where(even, 1, RING), slot]).astype(jnp.int32)
    sigma_now = sigma_of(window_steps[slot], 2 * slots)
    step_size = sigma_of(window_steps[slot + 1], 2 * slots) - sigma_now
    level = jnp.stack([sigma_now, step_size])

    places, end = layout()
    starts = [0] + [kp for kp, _ in places[1:]] + [end]
    landed = first_hop(place, queries[0], keys[0], values[0])
    received = [second_hop(landed, start, stop) for start, stop in zip(starts, starts[1:])]
    acc = None
    for number, ((k0, k1), (kp, vp)) in enumerate(zip(KEY_CUTS, places)):
        start = starts[number]
        last = number == len(KEY_CUTS) - 1
        got = attend(place, received[0], received[number], acc, k1 - k0, kp - start, vp - start, last)
        acc = None if last else got[0]
    ahead = (lax.broadcasted_iota(jnp.int32, (SLOTS // 2, LAT, QROWS), 0) > slot // 2).astype(jnp.float32)
    from_other = jnp.broadcast_to(jnp.where(even, 0.0, 1.0), (LAT, QROWS))
    got, ahead, from_other, *operands = lax.optimization_barrier(
        (got[0], ahead, from_other, level, hidden[0], w_proj, w_final.T, gate_base[None], gate_slope[None])
    )
    got = lax.all_to_all(got, "seq", 0, 0, tiled=True)
    velocity, drift = project(place, operands[0], got, *operands[1:])
    other = lax.ppermute(drift, "tm", [(i, i ^ 1) for i in range(SLOTS)])
    later = (ahead * (drift + other)[None]).astype(jnp.bfloat16)
    groups = [[core + 2 * chip for chip in range(SLOTS // 2)] for core in range(2)]
    earlier = lax.all_to_all(later, "tm", 0, 0, axis_index_groups=groups, tiled=True).astype(jnp.float32)
    latents = start_latent.T + drift + from_other * other + jnp.sum(earlier, axis=0)
    return (velocity.T[None], latents.T[None])


def solution(mesh):
    placed = (
        P("tm", "seq", None),
        P("tm", "seq", None),
        P("tm", "seq", None),
        P("tm", "seq", None),
        P(),
        P(),
        P(),
        P(),
        P("seq", None),
        P(),
    )
    return jax.shard_map(
        per_device,
        mesh=mesh,
        in_specs=placed,
        out_specs=(P("tm", "seq", None), P("tm", "seq", None)),
        check_vma=False,
    )
```

```python
import functools

import jax
import jax.numpy as jnp
from jax import lax
from jax.experimental import pallas as pl
from jax.experimental.pallas import tpu as pltpu
from jax.sharding import PartitionSpec as P

HEADS = 32
HEAD_DIM = 64
HD = 2048
D = 2432
LAT = 64
PAIR = 128
RING = 4
SLOTS = 8
BOTH = ("tm", "seq")
NT = (((1,), (1,)), ((), ()))
SCALE = 0.125 * 1.4426950408889634
KEY_CUTS = ((0, 80), (80, 280))
QROWS = 256
KROWS = 280
TILE = 512
BLOCK_Q = 2048
VROWS = 128
MIB = 2**20


def ring_perm(first, shift):
    pairs = []
    for slot in range(8):
        for place in range(16):
            x, z = divmod(place, RING)
            if (slot % 2 == 0) == first:
                x2, z2 = (x + shift) % RING, z
            else:
                x2, z2 = x, (z + shift) % RING
            pairs.append((slot * 16 + place, slot * 16 + x2 * RING + z2))
    return pairs


def send(value, first, shift):
    return lax.ppermute(value, BOTH, ring_perm(first, shift % RING))


def head_norm(block):
    wide = block.astype(jnp.float32)
    square = wide * wide
    high = square.astype(jnp.bfloat16)
    low = (square - high.astype(jnp.float32)).astype(jnp.bfloat16)
    row = lax.broadcasted_iota(jnp.int32, (PAIR, PAIR), 0)
    col = lax.broadcasted_iota(jnp.int32, (PAIR, PAIR), 1)
    same = ((row < HEAD_DIM) == (col < HEAD_DIM)).astype(jnp.bfloat16)
    total = jnp.dot(high, same, preferred_element_type=jnp.float32)
    total = total + jnp.dot(low, same, preferred_element_type=jnp.float32)
    return (wide * lax.rsqrt(total * (1.0 / HEAD_DIM) + 1e-06)).astype(jnp.bfloat16)


def padded(rows):
    return -(-rows // 16) * 16


def layout():
    at, places = QROWS, []
    for k0, k1 in KEY_CUTS:
        places.append((at, at + padded(k1 - k0)))
        at += 2 * padded(k1 - k0)
    return places, at


def pack_kernel(shifts, place_ref, q_hbm, k_hbm, v_hbm, *refs):
    outs, (q_buf, k_buf, v_buf, sems) = refs[: len(shifts)], refs[len(shifts) :]
    places, _ = layout()
    copies = []
    for i, d in enumerate(shifts):
        group = lax.rem(place_ref[0] + d, RING)
        lanes = pl.ds(pl.multiple_of(group * (RING * PAIR), RING * PAIR), RING * PAIR)
        copies.append(
            [
                pltpu.make_async_copy(source.at[:, lanes], target.at[i], sems.at[i, n])
                for n, (source, target) in enumerate(((q_hbm, q_buf), (k_hbm, k_buf), (v_hbm, v_buf)))
            ]
        )
        for copy in copies[i]:
            copy.start()
    for i in range(len(shifts)):
        for copy in copies[i]:
            copy.wait()
        out = outs[i]
        for e in range(RING):
            pair = lax.rem(place_ref[1] + e, RING)
            lanes = pl.ds(pl.multiple_of(pair * PAIR, PAIR), PAIR)
            out[e, 0:QROWS] = head_norm(q_buf[i, :, lanes])
            keys = head_norm(k_buf[i, :, lanes])
            for (k0, k1), (kp, vp) in zip(KEY_CUTS, places):
                out[e, kp : kp + k1 - k0] = keys[k0:k1]
                out[e, vp : vp + k1 - k0] = v_buf[i, k0:k1, lanes]
                gap = padded(k1 - k0) - (k1 - k0)
                if gap:
                    out[e, vp - gap : vp] = jnp.zeros((gap, PAIR), jnp.bfloat16)
                    out[e, vp + k1 - k0 : vp + k1 - k0 + gap] = jnp.zeros((gap, PAIR), jnp.bfloat16)


def pack(place, queries, keys, values, shifts):
    _, rows = layout()
    vmem = pl.BlockSpec(memory_space=pltpu.VMEM)
    wide = RING * PAIR
    count = len(shifts)
    return pl.pallas_call(
        functools.partial(pack_kernel, shifts),
        in_specs=[pl.BlockSpec(memory_space=pltpu.SMEM)] + [pl.BlockSpec(memory_space=pltpu.HBM)] * 3,
        out_specs=[vmem] * count,
        out_shape=[jax.ShapeDtypeStruct((RING, rows, PAIR), jnp.bfloat16)] * count,
        scratch_shapes=[
            pltpu.VMEM((count, QROWS, wide), jnp.bfloat16),
            pltpu.VMEM((count, KROWS, wide), jnp.bfloat16),
            pltpu.VMEM((count, KROWS, wide), jnp.bfloat16),
            pltpu.SemaphoreType.DMA((count, 3)),
        ],
        compiler_params=pltpu.CompilerParams(vmem_limit_bytes=59 * MIB),
        cost_estimate=pl.CostEstimate(
            flops=count * rows * HD * PAIR, bytes_accessed=count * rows * HD, transcendentals=0
        ),
        name="pack",
    )(place, queries, keys, values)


def first_hop(place, queries, keys, values):
    up, down, across, own = pack(place, queries, keys, values, (1, 3, 2, 0))
    return [own, send(up, True, 1), send(across, True, 2), send(down, True, 3)]


def second_hop(landed, start, stop):
    staged = [jnp.stack([part[e, start:stop] for part in landed]) for e in range(RING)]
    return [staged[0]] + [send(staged[e], False, e) for e in range(1, RING)]


def cuts_of(total, step):
    return [(start, min(step, total - start)) for start in range(0, total, step)]


def attend_kernel(count, q_from, key_from, groups, before, last, place_ref, *refs):
    parts, refs = refs[:count], refs[count:]
    if before:
        acc, refs = refs[0], refs[1:]
    result, q_all, k_all, low_t, high_t = refs
    nr = QROWS
    row = lax.broadcasted_iota(jnp.int32, (PAIR, PAIR), 0)
    col = lax.broadcasted_iota(jnp.int32, (PAIR, PAIR), 1)
    eye = (row == col).astype(jnp.bfloat16)
    for i, source in enumerate(q_from):
        for d in range(RING):
            slot = i * RING + d
            q_all[slot * nr : (slot + 1) * nr] = parts[source][d, 0:nr]
    low_t[HEAD_DIM:, :] = jnp.ones((VROWS - HEAD_DIM, low_t.shape[1]), jnp.bfloat16)
    high_t[HEAD_DIM:, :] = jnp.ones((VROWS - HEAD_DIM, low_t.shape[1]), jnp.bfloat16)
    at = 0
    for source, kp, vp, nk in key_from:
        part = parts[source]
        for d in range(RING):
            k_all[at + d * nk : at + (d + 1) * nk] = part[d, kp : kp + nk]
        joined = jnp.concatenate([part[d, vp : vp + nk] for d in range(RING)], axis=0)
        turned = lax.dot_general(eye, joined, NT, preferred_element_type=jnp.float32).astype(jnp.bfloat16)
        low_t[0:HEAD_DIM, at : at + RING * nk] = turned[:HEAD_DIM]
        high_t[0:HEAD_DIM, at : at + RING * nk] = turned[HEAD_DIM:]
        at += RING * nk
    values_t = (low_t, high_t)
    kept = HEAD_DIM + 8
    for block, (lowest, highest) in enumerate(groups):
        rows = slice(block * BLOCK_Q, (block + 1) * BLOCK_Q)
        work = [(h, lowest + start, size) for start, size in cuts_of(highest - lowest, TILE) for h in range(2)]
        q = q_all[rows, :]
        lane = lax.broadcasted_iota(jnp.int32, q.shape, 1)
        zero = jnp.zeros_like(q)
        halves = (jnp.where(lane < HEAD_DIM, q, zero), jnp.where(lane < HEAD_DIM, zero, q))
        sums = [jnp.zeros((VROWS, BLOCK_Q), jnp.float32) for _ in range(2)]

        def score(item):
            h, start, size = item
            return lax.dot_general(k_all[start : start + size, :], halves[h], NT, preferred_element_type=jnp.float32)

        ahead = score(work[0])
        for i, (h, start, size) in enumerate(work):
            now = ahead
            if i + 1 < len(work):
                ahead = score(work[i + 1])
            weights = jnp.exp2(now * SCALE).astype(jnp.bfloat16)
            sums[h] = sums[h] + jnp.dot(
                values_t[h][:, start : start + size], weights, preferred_element_type=jnp.float32
            )
        sums = [part[:kept] for part in sums]
        if block < before:
            sums = [part + acc[h, :, rows] for h, part in enumerate(sums)]
        if not last:
            for h in range(2):
                result[h, :, rows] = sums[h]
        else:
            done = jnp.concatenate([part[:HEAD_DIM] / part[HEAD_DIM : HEAD_DIM + 1] for part in sums], axis=0)
            q_all[rows, :] = done.T.astype(jnp.bfloat16)

    if last:
        for e in range(RING):
            for d in range(RING):
                slot = e * RING + d
                along = lax.rem(place_ref[0] + RING - d, RING)
                across = lax.rem(place_ref[1] + RING - e, RING)
                result[along * place_ref[2] + across * place_ref[3]] = q_all[slot * nr : (slot + 1) * nr]


def attend(place, parts, q_from, key_from, groups, acc=None, last=False):
    nq = len(q_from) * RING * QROWS
    total = sum(RING * nk for _, _, _, nk in key_from)
    before = 0 if acc is None else acc.shape[2] // BLOCK_Q
    operands = list(parts) + ([] if acc is None else [acc])
    vmem = pl.BlockSpec(memory_space=pltpu.VMEM)
    if last:
        out_shape = jax.ShapeDtypeStruct((RING * RING, QROWS, PAIR), jnp.bfloat16)
    else:
        out_shape = jax.ShapeDtypeStruct((2, HEAD_DIM + 8, nq), jnp.float32)
    keys = sum(high - low for low, high in groups)
    return pl.pallas_call(
        functools.partial(attend_kernel, len(parts), q_from, key_from, groups, before, last),
        in_specs=[pl.BlockSpec(memory_space=pltpu.SMEM)] + [vmem] * len(operands),
        out_specs=vmem,
        out_shape=out_shape,
        scratch_shapes=[
            pltpu.VMEM((nq, PAIR), jnp.bfloat16),
            pltpu.VMEM((total, PAIR), jnp.bfloat16),
            pltpu.VMEM((VROWS, total), jnp.bfloat16),
            pltpu.VMEM((VROWS, total), jnp.bfloat16),
        ],
        compiler_params=pltpu.CompilerParams(vmem_limit_bytes=32 * MIB),
        cost_estimate=pl.CostEstimate(
            flops=2 * 2 * 4 * BLOCK_Q * keys * PAIR, bytes_accessed=2 * MIB, transcendentals=2 * BLOCK_Q * keys
        ),
        name="attend",
    )(place, *operands)


def project_kernel(place_ref, level_ref, got_ref, hidden_ref, w_proj_ref, w_final_ref, base_ref, slope_ref, *refs):
    velocity_ref, drift_ref, joined = refs
    for j in range(RING * RING):
        hi, lo = divmod(j, RING)
        pair = hi * place_ref[2] + lo * place_ref[3]
        joined[:, pl.ds(pl.multiple_of(pair * PAIR, PAIR), PAIR)] = got_ref[j]
    squares = jnp.zeros((QROWS, 1), jnp.float32)
    product = jnp.zeros((LAT, QROWS), jnp.float32)
    for start, size in cuts_of(D, 512):
        cols = slice(start, start + size)
        projected = jnp.dot(joined[...], w_proj_ref[:, cols], preferred_element_type=jnp.float32)
        gate = base_ref[:, cols] + level_ref[0] * slope_ref[:, cols]
        value = hidden_ref[:, cols].astype(jnp.float32) + gate * projected
        product = product + lax.dot_general(
            w_final_ref[:, cols], value.astype(jnp.bfloat16), NT, preferred_element_type=jnp.float32
        )
        squares = squares + jnp.sum(value * value, axis=1, keepdims=True)
    along = jnp.broadcast_to(squares, (QROWS, PAIR)).T[0:1]
    velocity = product * lax.rsqrt(along * (1.0 / D) + 1e-06)
    velocity_ref[...] = velocity
    drift = velocity * level_ref[1]
    drift_ref[...] = drift


def project(place, level, got, hidden, w_proj, w_final, base, slope):
    vmem = pl.BlockSpec(memory_space=pltpu.VMEM)
    smem = pl.BlockSpec(memory_space=pltpu.SMEM)
    return pl.pallas_call(
        project_kernel,
        in_specs=[smem, smem] + [vmem] * 6,
        out_specs=[vmem] * 2,
        out_shape=[
            jax.ShapeDtypeStruct((LAT, QROWS), jnp.float32),
            jax.ShapeDtypeStruct((LAT, QROWS), jnp.float32),
        ],
        scratch_shapes=[pltpu.VMEM((QROWS, HD), jnp.bfloat16)],
        compiler_params=pltpu.CompilerParams(vmem_limit_bytes=16 * MIB),
        cost_estimate=pl.CostEstimate(flops=2 * QROWS * HD * D, bytes_accessed=12 * MIB, transcendentals=0),
        name="project",
    )(place, level, got, hidden, w_proj, w_final, base, slope)


def sigma_of(index_val, total_steps):
    frac = 1.0 - index_val.astype(jnp.float32) / total_steps
    return 3.0 * frac / (1.0 + 2.0 * frac)


def per_device(
    queries, keys, values, hidden, w_proj, w_final, gate_base, gate_slope, start_latent, window_steps
):
    slots = lax.axis_size("tm")
    slot = lax.axis_index("tm")
    seat = lax.axis_index("seq")
    x, z = seat // RING, lax.rem(seat, RING)
    even = lax.rem(slot, 2) == 0
    first, second = jnp.where(even, x, z), jnp.where(even, z, x)
    place = jnp.stack([first, second, jnp.where(even, RING, 1), jnp.where(even, 1, RING), slot]).astype(jnp.int32)
    sigma_now = sigma_of(window_steps[slot], 2 * slots)
    step_size = sigma_of(window_steps[slot + 1], 2 * slots) - sigma_now
    level = jnp.stack([sigma_now, step_size])

    places, end = layout()
    starts = [0] + [kp for kp, _ in places[1:]] + [end]
    landed = first_hop(place, queries[0], keys[0], values[0])
    received = [second_hop(landed, start, stop) for start, stop in zip(starts, starts[1:])]
    (a0, a1), (b0, b1) = KEY_CUTS
    na, nb = a1 - a0, b1 - b0
    kb, vb = places[1][0] - starts[1], places[1][1] - starts[1]
    first_part, second_part = received
    in_a = [(e, *places[0], na) for e in range(RING)]
    acc = attend(
        place,
        [first_part[0], first_part[1], second_part[0]],
        (0, 1),
        (*in_a[:2], (2, kb, vb, nb)),
        ((0, RING * (2 * na + nb)),),
    )
    acc = attend(
        place, first_part, range(RING), in_a, ((2 * RING * na, RING * RING * na), (0, RING * RING * na)), acc
    )
    got = attend(
        place,
        [*first_part, *second_part],
        range(RING),
        [(RING + e, kb, vb, nb) for e in range(RING)],
        ((RING * nb, RING * RING * nb), (0, RING * RING * nb)),
        acc,
        True,
    )
    ahead = (lax.broadcasted_iota(jnp.int32, (SLOTS // 2, LAT, QROWS), 0) > slot // 2).astype(jnp.float32)
    from_other = jnp.broadcast_to(jnp.where(even, 0.0, 1.0), (LAT, QROWS))
    got, ahead, from_other, *operands = lax.optimization_barrier(
        (got, ahead, from_other, level, hidden[0], w_proj, w_final.T, gate_base[None], gate_slope[None])
    )
    got = lax.all_to_all(got, "seq", 0, 0, tiled=True)
    velocity, drift = project(place, operands[0], got, *operands[1:])
    other = lax.ppermute(drift, "tm", [(i, i ^ 1) for i in range(SLOTS)])
    later = (ahead * (drift + other)[None]).astype(jnp.bfloat16)
    groups = [[core + 2 * chip for chip in range(SLOTS // 2)] for core in range(2)]
    earlier = lax.all_to_all(later, "tm", 0, 0, axis_index_groups=groups, tiled=True).astype(jnp.float32)
    latents = start_latent.T + drift + from_other * other + jnp.sum(earlier, axis=0)
    return (velocity.T[None], latents.T[None])


def solution(mesh):
    placed = (
        P("tm", "seq", None),
        P("tm", "seq", None),
        P("tm", "seq", None),
        P("tm", "seq", None),
        P(),
        P(),
        P(),
        P(),
        P("seq", None),
        P(),
    )
    return jax.shard_map(
        per_device,
        mesh=mesh,
        in_specs=placed,
        out_specs=(P("tm", "seq", None), P("tm", "seq", None)),
        check_vma=False,
    )
```

```python
import functools

import jax
import jax.numpy as jnp
from jax import lax
from jax.experimental import pallas as pl
from jax.experimental.pallas import tpu as pltpu
from jax.sharding import PartitionSpec as P

HEADS = 32
HEAD_DIM = 64
HD = 2048
D = 2432
LAT = 64
PAIR = 128
RING = 4
SLOTS = 8
BOTH = ("tm", "seq")
NT = (((1,), (1,)), ((), ()))
SCALE = 0.125 * 1.4426950408889634
KEY_CUTS = ((0, 96), (96, 280))
QROWS = 256
KROWS = 280
TILE = 512
BLOCK_Q = 2048
VROWS = 128
MIB = 2**20


def swap_pairs(first, mask):
    pairs = []
    for slot in range(8):
        for place in range(16):
            x, z = divmod(place, RING)
            if (slot % 2 == 0) == first:
                x2, z2 = x ^ mask, z
            else:
                x2, z2 = x, z ^ mask
            pairs.append((slot * 16 + place, slot * 16 + x2 * RING + z2))
    return pairs


def send(value, first, mask):
    return lax.ppermute(value, BOTH, swap_pairs(first, mask))


def head_norm(block):
    wide = block.astype(jnp.float32)
    square = wide * wide
    high = square.astype(jnp.bfloat16)
    low = (square - high.astype(jnp.float32)).astype(jnp.bfloat16)
    row = lax.broadcasted_iota(jnp.int32, (PAIR, PAIR), 0)
    col = lax.broadcasted_iota(jnp.int32, (PAIR, PAIR), 1)
    same = ((row < HEAD_DIM) == (col < HEAD_DIM)).astype(jnp.bfloat16)
    total = jnp.dot(high, same, preferred_element_type=jnp.float32)
    total = total + jnp.dot(low, same, preferred_element_type=jnp.float32)
    return (wide * lax.rsqrt(total * (1.0 / HEAD_DIM) + 1e-06)).astype(jnp.bfloat16)


def padded(rows):
    return -(-rows // 16) * 16


def layout():
    at, places = QROWS, []
    for k0, k1 in KEY_CUTS:
        places.append((at, at + padded(k1 - k0)))
        at += 2 * padded(k1 - k0)
    return places, at


def pack_kernel(shifts, q_hbm, k_hbm, v_hbm, *refs):
    seat, odd = lax.axis_index("seq"), lax.rem(lax.axis_index("tm"), 2)
    x, z = seat // RING, lax.rem(seat, RING)
    first, second = x + odd * (z - x), z + odd * (x - z)
    outs, (q_buf, k_buf, v_buf, sems) = refs[: len(shifts)], refs[len(shifts) :]
    places, _ = layout()
    copies = []
    for i, d in enumerate(shifts):
        group = first ^ d
        lanes = pl.ds(pl.multiple_of(group * (RING * PAIR), RING * PAIR), RING * PAIR)
        copies.append(
            [
                pltpu.make_async_copy(source.at[:, lanes], target.at[i], sems.at[i, n])
                for n, (source, target) in enumerate(((q_hbm, q_buf), (k_hbm, k_buf), (v_hbm, v_buf)))
            ]
        )
        for copy in copies[i]:
            copy.start()
    for i in range(len(shifts)):
        for copy in copies[i]:
            copy.wait()
        out = outs[i]
        for e in range(RING):
            pair = second ^ e
            lanes = pl.ds(pl.multiple_of(pair * PAIR, PAIR), PAIR)
            out[e, 0:QROWS] = head_norm(q_buf[i, :, lanes])
            keys = head_norm(k_buf[i, :, lanes])
            for (k0, k1), (kp, vp) in zip(KEY_CUTS, places):
                out[e, kp : kp + k1 - k0] = keys[k0:k1]
                out[e, vp : vp + k1 - k0] = v_buf[i, k0:k1, lanes]
                gap = padded(k1 - k0) - (k1 - k0)
                if gap:
                    out[e, vp - gap : vp] = jnp.zeros((gap, PAIR), jnp.bfloat16)
                    out[e, vp + k1 - k0 : vp + k1 - k0 + gap] = jnp.zeros((gap, PAIR), jnp.bfloat16)


def pack(queries, keys, values, shifts):
    _, rows = layout()
    vmem = pl.BlockSpec(memory_space=pltpu.VMEM)
    wide = RING * PAIR
    count = len(shifts)
    return pl.pallas_call(
        functools.partial(pack_kernel, shifts),
        in_specs=[pl.BlockSpec(memory_space=pltpu.HBM)] * 3,
        out_specs=[vmem] * count,
        out_shape=[jax.ShapeDtypeStruct((RING, rows, PAIR), jnp.bfloat16)] * count,
        scratch_shapes=[
            pltpu.VMEM((count, QROWS, wide), jnp.bfloat16),
            pltpu.VMEM((count, KROWS, wide), jnp.bfloat16),
            pltpu.VMEM((count, KROWS, wide), jnp.bfloat16),
            pltpu.SemaphoreType.DMA((count, 3)),
        ],
        compiler_params=pltpu.CompilerParams(vmem_limit_bytes=59 * MIB),
        cost_estimate=pl.CostEstimate(
            flops=count * rows * HD * PAIR, bytes_accessed=count * rows * HD, transcendentals=0
        ),
        name="pack",
    )(queries, keys, values)


def first_hop(queries, keys, values):
    up, down, across, own = pack(queries, keys, values, (1, 3, 2, 0))
    return [own, send(up, True, 1), send(across, True, 2), send(down, True, 3)]


def second_hop(landed, start, stop):
    staged = [jnp.stack([part[e, start:stop] for part in landed]) for e in range(RING)]
    return [staged[0]] + [send(staged[e], False, e) for e in range(1, RING)]


def cuts_of(total, step):
    return [(start, min(step, total - start)) for start in range(0, total, step)]


def attend_kernel(count, q_from, key_from, groups, before, last, place_ref, *refs):
    parts, refs = refs[:count], refs[count:]
    if before:
        acc, refs = refs[0], refs[1:]
    result, q_all, k_all, low_t, high_t = refs
    nr = QROWS
    row = lax.broadcasted_iota(jnp.int32, (PAIR, PAIR), 0)
    col = lax.broadcasted_iota(jnp.int32, (PAIR, PAIR), 1)
    eye = (row == col).astype(jnp.bfloat16)
    for i, source in enumerate(q_from):
        for d in range(RING):
            slot = i * RING + d
            q_all[slot * nr : (slot + 1) * nr] = parts[source][d, 0:nr]
    low_t[HEAD_DIM:, :] = jnp.ones((VROWS - HEAD_DIM, low_t.shape[1]), jnp.bfloat16)
    high_t[HEAD_DIM:, :] = jnp.ones((VROWS - HEAD_DIM, low_t.shape[1]), jnp.bfloat16)
    at = 0
    for source, kp, vp, nk in key_from:
        part = parts[source]
        for d in range(RING):
            k_all[at + d * nk : at + (d + 1) * nk] = part[d, kp : kp + nk]
        joined = jnp.concatenate([part[d, vp : vp + nk] for d in range(RING)], axis=0)
        turned = lax.dot_general(eye, joined, NT, preferred_element_type=jnp.float32).astype(jnp.bfloat16)
        low_t[0:HEAD_DIM, at : at + RING * nk] = turned[:HEAD_DIM]
        high_t[0:HEAD_DIM, at : at + RING * nk] = turned[HEAD_DIM:]
        at += RING * nk
    values_t = (low_t, high_t)
    kept = HEAD_DIM + 8
    for block, (lowest, highest) in enumerate(groups):
        rows = slice(block * BLOCK_Q, (block + 1) * BLOCK_Q)
        work = [(h, lowest + start, size) for start, size in cuts_of(highest - lowest, TILE) for h in range(2)]
        q = q_all[rows, :]
        lane = lax.broadcasted_iota(jnp.int32, q.shape, 1)
        zero = jnp.zeros_like(q)
        halves = (jnp.where(lane < HEAD_DIM, q, zero), jnp.where(lane < HEAD_DIM, zero, q))
        sums = [jnp.zeros((VROWS, BLOCK_Q), jnp.float32) for _ in range(2)]

        def score(item):
            h, start, size = item
            return lax.dot_general(k_all[start : start + size, :], halves[h], NT, preferred_element_type=jnp.float32)

        ahead = score(work[0])
        for i, (h, start, size) in enumerate(work):
            now = ahead
            if i + 1 < len(work):
                ahead = score(work[i + 1])
            weights = jnp.exp2(now * SCALE).astype(jnp.bfloat16)
            sums[h] = sums[h] + jnp.dot(
                values_t[h][:, start : start + size], weights, preferred_element_type=jnp.float32
            )
        sums = [part[:kept] for part in sums]
        if block < before:
            sums = [part + acc[h, :, rows] for h, part in enumerate(sums)]
        if not last:
            for h in range(2):
                result[h, :, rows] = sums[h]
        else:
            done = jnp.concatenate([part[:HEAD_DIM] / part[HEAD_DIM : HEAD_DIM + 1] for part in sums], axis=0)
            q_all[rows, :] = done.T.astype(jnp.bfloat16)

    if last:
        for e in range(RING):
            for d in range(RING):
                slot = e * RING + d
                along = place_ref[0] ^ d
                across = place_ref[1] ^ e
                result[along * place_ref[2] + across * place_ref[3]] = q_all[slot * nr : (slot + 1) * nr]


def attend(place, parts, q_from, key_from, groups, acc=None, last=False):
    nq = len(q_from) * RING * QROWS
    total = sum(RING * nk for _, _, _, nk in key_from)
    before = 0 if acc is None else acc.shape[2] // BLOCK_Q
    operands = list(parts) + ([] if acc is None else [acc])
    vmem = pl.BlockSpec(memory_space=pltpu.VMEM)
    if last:
        out_shape = jax.ShapeDtypeStruct((RING * RING, QROWS, PAIR), jnp.bfloat16)
    else:
        out_shape = jax.ShapeDtypeStruct((2, HEAD_DIM + 8, nq), jnp.float32)
    keys = sum(high - low for low, high in groups)
    return pl.pallas_call(
        functools.partial(attend_kernel, len(parts), q_from, key_from, groups, before, last),
        in_specs=[pl.BlockSpec(memory_space=pltpu.SMEM)] + [vmem] * len(operands),
        out_specs=vmem,
        out_shape=out_shape,
        scratch_shapes=[
            pltpu.VMEM((nq, PAIR), jnp.bfloat16),
            pltpu.VMEM((total, PAIR), jnp.bfloat16),
            pltpu.VMEM((VROWS, total), jnp.bfloat16),
            pltpu.VMEM((VROWS, total), jnp.bfloat16),
        ],
        compiler_params=pltpu.CompilerParams(vmem_limit_bytes=32 * MIB),
        cost_estimate=pl.CostEstimate(
            flops=2 * 2 * 4 * BLOCK_Q * keys * PAIR, bytes_accessed=2 * MIB, transcendentals=2 * BLOCK_Q * keys
        ),
        name="attend",
    )(place, *operands)


def project_kernel(place_ref, level_ref, got_ref, hidden_ref, w_proj_ref, w_final_ref, base_ref, slope_ref, *refs):
    velocity_ref, drift_ref, joined = refs
    for j in range(RING * RING):
        hi, lo = divmod(j, RING)
        pair = hi * place_ref[2] + lo * place_ref[3]
        joined[:, pl.ds(pl.multiple_of(pair * PAIR, PAIR), PAIR)] = got_ref[j]
    squares = jnp.zeros((QROWS, 1), jnp.float32)
    product = jnp.zeros((LAT, QROWS), jnp.float32)
    for start, size in cuts_of(D, 512):
        cols = slice(start, start + size)
        projected = jnp.dot(joined[...], w_proj_ref[:, cols], preferred_element_type=jnp.float32)
        gate = base_ref[:, cols] + level_ref[0] * slope_ref[:, cols]
        value = hidden_ref[:, cols].astype(jnp.float32) + gate * projected
        product = product + lax.dot_general(
            w_final_ref[:, cols], value.astype(jnp.bfloat16), NT, preferred_element_type=jnp.float32
        )
        squares = squares + jnp.sum(value * value, axis=1, keepdims=True)
    along = jnp.broadcast_to(squares, (QROWS, PAIR)).T[0:1]
    velocity = product * lax.rsqrt(along * (1.0 / D) + 1e-06)
    velocity_ref[...] = velocity
    drift = velocity * level_ref[1]
    drift_ref[...] = drift


def project(place, level, got, hidden, w_proj, w_final, base, slope):
    vmem = pl.BlockSpec(memory_space=pltpu.VMEM)
    smem = pl.BlockSpec(memory_space=pltpu.SMEM)
    return pl.pallas_call(
        project_kernel,
        in_specs=[smem, smem] + [vmem] * 6,
        out_specs=[vmem] * 2,
        out_shape=[
            jax.ShapeDtypeStruct((LAT, QROWS), jnp.float32),
            jax.ShapeDtypeStruct((LAT, QROWS), jnp.float32),
        ],
        scratch_shapes=[pltpu.VMEM((QROWS, HD), jnp.bfloat16)],
        compiler_params=pltpu.CompilerParams(vmem_limit_bytes=16 * MIB),
        cost_estimate=pl.CostEstimate(flops=2 * QROWS * HD * D, bytes_accessed=12 * MIB, transcendentals=0),
        name="project",
    )(place, level, got, hidden, w_proj, w_final, base, slope)


def sigma_of(index_val, total_steps):
    frac = 1.0 - index_val.astype(jnp.float32) / total_steps
    return 3.0 * frac / (1.0 + 2.0 * frac)


def per_device(
    queries, keys, values, hidden, w_proj, w_final, gate_base, gate_slope, start_latent, window_steps
):
    slots = lax.axis_size("tm")
    slot = lax.axis_index("tm")
    seat = lax.axis_index("seq")
    x, z = seat // RING, lax.rem(seat, RING)
    even = lax.rem(slot, 2) == 0
    first, second = jnp.where(even, x, z), jnp.where(even, z, x)
    place = jnp.stack([first, second, jnp.where(even, RING, 1), jnp.where(even, 1, RING), slot]).astype(jnp.int32)
    sigma_now = sigma_of(window_steps[slot], 2 * slots)
    step_size = sigma_of(window_steps[slot + 1], 2 * slots) - sigma_now
    level = jnp.stack([sigma_now, step_size])

    places, end = layout()
    starts = [0] + [kp for kp, _ in places[1:]] + [end]
    landed = first_hop(queries[0], keys[0], values[0])
    received = [second_hop(landed, start, stop) for start, stop in zip(starts, starts[1:])]
    (a0, a1), (b0, b1) = KEY_CUTS
    na, nb = a1 - a0, b1 - b0
    kb, vb = places[1][0] - starts[1], places[1][1] - starts[1]
    first_part, second_part = received
    in_a = [(e, *places[0], na) for e in range(RING)]
    acc = attend(
        place,
        [first_part[0], first_part[1], second_part[0]],
        (0, 1),
        (*in_a[:2], (2, kb, vb, nb)),
        ((0, RING * (2 * na + nb)),),
    )
    acc = attend(
        place, first_part, range(RING), in_a, ((2 * RING * na, RING * RING * na), (0, RING * RING * na)), acc
    )
    got = attend(
        place,
        [*first_part, *second_part],
        range(RING),
        [(RING + e, kb, vb, nb) for e in range(RING)],
        ((RING * nb, RING * RING * nb), (0, RING * RING * nb)),
        acc,
        True,
    )
    ahead = (lax.broadcasted_iota(jnp.int32, (SLOTS // 2, LAT, QROWS), 0) > slot // 2).astype(jnp.float32)
    from_other = jnp.broadcast_to(jnp.where(even, 0.0, 1.0), (LAT, QROWS))
    got, ahead, from_other, *operands = lax.optimization_barrier(
        (got, ahead, from_other, level, hidden[0], w_proj, w_final.T, gate_base[None], gate_slope[None])
    )
    got = lax.all_to_all(got, "seq", 0, 0, tiled=True)
    velocity, drift = project(place, operands[0], got, *operands[1:])
    other = lax.ppermute(drift, "tm", [(i, i ^ 1) for i in range(SLOTS)])
    later = (ahead * (drift + other)[None]).astype(jnp.bfloat16)
    groups = [[core + 2 * chip for chip in range(SLOTS // 2)] for core in range(2)]
    earlier = lax.all_to_all(later, "tm", 0, 0, axis_index_groups=groups, tiled=True).astype(jnp.float32)
    latents = start_latent.T + drift + from_other * other + jnp.sum(earlier, axis=0)
    return (velocity.T[None], latents.T[None])


def solution(mesh):
    placed = (
        P("tm", "seq", None),
        P("tm", "seq", None),
        P("tm", "seq", None),
        P("tm", "seq", None),
        P(),
        P(),
        P(),
        P(),
        P("seq", None),
        P(),
    )
    return jax.shard_map(
        per_device,
        mesh=mesh,
        in_specs=placed,
        out_specs=(P("tm", "seq", None), P("tm", "seq", None)),
        check_vma=False,
    )
```

```python
import functools

import jax
import jax.numpy as jnp
from jax import lax
from jax.experimental import pallas as pl
from jax.experimental.pallas import tpu as pltpu
from jax.sharding import PartitionSpec as P

HEADS = 32
HEAD_DIM = 64
HD = 2048
D = 2432
LAT = 64
PAIR = 128
RING = 4
SLOTS = 8
BOTH = ("tm", "seq")
NT = (((1,), (1,)), ((), ()))
SCALE = 0.125 * 1.4426950408889634
KEY_CUTS = ((0, 96), (96, 280))
QROWS = 256
KROWS = 280
TILE = 512
BLOCK_Q = 2048
STEP_Q = 1024
VROWS = 128
MIB = 2**20


def swap_pairs(first, mask):
    pairs = []
    for slot in range(8):
        for place in range(16):
            x, z = divmod(place, RING)
            if (slot % 2 == 0) == first:
                x2, z2 = x ^ mask, z
            else:
                x2, z2 = x, z ^ mask
            pairs.append((slot * 16 + place, slot * 16 + x2 * RING + z2))
    return pairs


def send(value, first, mask):
    return lax.ppermute(value, BOTH, swap_pairs(first, mask))


def head_norm(block):
    wide = block.astype(jnp.float32)
    square = wide * wide
    high = square.astype(jnp.bfloat16)
    low = (square - high.astype(jnp.float32)).astype(jnp.bfloat16)
    row = lax.broadcasted_iota(jnp.int32, (PAIR, PAIR), 0)
    col = lax.broadcasted_iota(jnp.int32, (PAIR, PAIR), 1)
    same = ((row < HEAD_DIM) == (col < HEAD_DIM)).astype(jnp.bfloat16)
    total = jnp.dot(high, same, preferred_element_type=jnp.float32)
    total = total + jnp.dot(low, same, preferred_element_type=jnp.float32)
    return (wide * lax.rsqrt(total * (1.0 / HEAD_DIM) + 1e-06)).astype(jnp.bfloat16)


def padded(rows):
    return -(-rows // 16) * 16


def layout():
    at, places = QROWS, []
    for k0, k1 in KEY_CUTS:
        places.append((at, at + padded(k1 - k0)))
        at += 2 * padded(k1 - k0)
    return places, at


def pack_kernel(shifts, q_hbm, k_hbm, v_hbm, *refs):
    seat, odd = lax.axis_index("seq"), lax.rem(lax.axis_index("tm"), 2)
    x, z = seat // RING, lax.rem(seat, RING)
    first, second = x + odd * (z - x), z + odd * (x - z)
    outs, (q_buf, k_buf, v_buf, sems) = refs[: len(shifts)], refs[len(shifts) :]
    places, _ = layout()
    copies = []
    for i, d in enumerate(shifts):
        group = first ^ d
        lanes = pl.ds(pl.multiple_of(group * (RING * PAIR), RING * PAIR), RING * PAIR)
        copies.append(
            [
                pltpu.make_async_copy(source.at[:, lanes], target.at[i], sems.at[i, n])
                for n, (source, target) in enumerate(((q_hbm, q_buf), (k_hbm, k_buf), (v_hbm, v_buf)))
            ]
        )
        for copy in copies[i]:
            copy.start()
    for i in range(len(shifts)):
        for copy in copies[i]:
            copy.wait()
        out = outs[i]
        for e in range(RING):
            pair = second ^ e
            lanes = pl.ds(pl.multiple_of(pair * PAIR, PAIR), PAIR)
            out[e, 0:QROWS] = head_norm(q_buf[i, :, lanes])
            keys = head_norm(k_buf[i, :, lanes])
            for (k0, k1), (kp, vp) in zip(KEY_CUTS, places):
                out[e, kp : kp + k1 - k0] = keys[k0:k1]
                out[e, vp : vp + k1 - k0] = v_buf[i, k0:k1, lanes]
                gap = padded(k1 - k0) - (k1 - k0)
                if gap:
                    out[e, vp - gap : vp] = jnp.zeros((gap, PAIR), jnp.bfloat16)
                    out[e, vp + k1 - k0 : vp + k1 - k0 + gap] = jnp.zeros((gap, PAIR), jnp.bfloat16)


def pack(queries, keys, values, shifts):
    _, rows = layout()
    vmem = pl.BlockSpec(memory_space=pltpu.VMEM)
    wide = RING * PAIR
    count = len(shifts)
    return pl.pallas_call(
        functools.partial(pack_kernel, shifts),
        in_specs=[pl.BlockSpec(memory_space=pltpu.HBM)] * 3,
        out_specs=[vmem] * count,
        out_shape=[jax.ShapeDtypeStruct((RING, rows, PAIR), jnp.bfloat16)] * count,
        scratch_shapes=[
            pltpu.VMEM((count, QROWS, wide), jnp.bfloat16),
            pltpu.VMEM((count, KROWS, wide), jnp.bfloat16),
            pltpu.VMEM((count, KROWS, wide), jnp.bfloat16),
            pltpu.SemaphoreType.DMA((count, 3)),
        ],
        compiler_params=pltpu.CompilerParams(vmem_limit_bytes=59 * MIB),
        cost_estimate=pl.CostEstimate(
            flops=count * rows * HD * PAIR, bytes_accessed=count * rows * HD, transcendentals=0
        ),
        name="pack",
    )(queries, keys, values)


def first_hop(queries, keys, values):
    up, down, across, own = pack(queries, keys, values, (1, 3, 2, 0))
    return [own, send(up, True, 1), send(across, True, 2), send(down, True, 3)]


def second_hop(landed, start, stop):
    staged = [jnp.stack([part[e, start:stop] for part in landed]) for e in range(RING)]
    return [staged[0]] + [send(staged[e], False, e) for e in range(1, RING)]


def cuts_of(total, step):
    return [(start, min(step, total - start)) for start in range(0, total, step)]


def attend_kernel(count, q_from, key_from, groups, before, last, place_ref, *refs):
    parts, refs = refs[:count], refs[count:]
    if before:
        acc, refs = refs[0], refs[1:]
    result, q_all, k_all, low_t, high_t = refs
    nr = QROWS
    row = lax.broadcasted_iota(jnp.int32, (PAIR, PAIR), 0)
    col = lax.broadcasted_iota(jnp.int32, (PAIR, PAIR), 1)
    eye = (row == col).astype(jnp.bfloat16)
    for i, source in enumerate(q_from):
        for d in range(RING):
            slot = i * RING + d
            q_all[slot * nr : (slot + 1) * nr] = parts[source][d, 0:nr]
    low_t[HEAD_DIM:, :] = jnp.ones((VROWS - HEAD_DIM, low_t.shape[1]), jnp.bfloat16)
    high_t[HEAD_DIM:, :] = jnp.ones((VROWS - HEAD_DIM, low_t.shape[1]), jnp.bfloat16)
    at = 0
    for source, kp, vp, nk in key_from:
        part = parts[source]
        for d in range(RING):
            k_all[at + d * nk : at + (d + 1) * nk] = part[d, kp : kp + nk]
        joined = jnp.concatenate([part[d, vp : vp + nk] for d in range(RING)], axis=0)
        turned = lax.dot_general(eye, joined, NT, preferred_element_type=jnp.float32).astype(jnp.bfloat16)
        low_t[0:HEAD_DIM, at : at + RING * nk] = turned[:HEAD_DIM]
        high_t[0:HEAD_DIM, at : at + RING * nk] = turned[HEAD_DIM:]
        at += RING * nk
    values_t = (low_t, high_t)
    kept = HEAD_DIM + 8
    for block, (lowest, highest) in enumerate(groups):
        work = [(h, lowest + start, size) for start, size in cuts_of(highest - lowest, TILE) for h in range(2)]

        @pl.loop(0, BLOCK_Q // STEP_Q)
        def _(step, block=block, work=work):
            rows = pl.ds(pl.multiple_of(block * BLOCK_Q + step * STEP_Q, STEP_Q), STEP_Q)
            q = q_all[rows, :]
            lane = lax.broadcasted_iota(jnp.int32, q.shape, 1)
            zero = jnp.zeros_like(q)
            halves = (jnp.where(lane < HEAD_DIM, q, zero), jnp.where(lane < HEAD_DIM, zero, q))
            sums = [jnp.zeros((VROWS, STEP_Q), jnp.float32) for _ in range(2)]

            def score(item):
                h, start, size = item
                return lax.dot_general(
                    k_all[start : start + size, :], halves[h], NT, preferred_element_type=jnp.float32
                )

            ahead = score(work[0])
            for i, (h, start, size) in enumerate(work):
                now = ahead
                if i + 1 < len(work):
                    ahead = score(work[i + 1])
                weights = jnp.exp2(now * SCALE).astype(jnp.bfloat16)
                sums[h] = sums[h] + jnp.dot(
                    values_t[h][:, start : start + size], weights, preferred_element_type=jnp.float32
                )
            sums = [part[:kept] for part in sums]
            if block < before:
                sums = [part + acc[h, :, rows] for h, part in enumerate(sums)]
            if not last:
                for h in range(2):
                    result[h, :, rows] = sums[h]
            else:
                done = jnp.concatenate([part[:HEAD_DIM] / part[HEAD_DIM : HEAD_DIM + 1] for part in sums], axis=0)
                q_all[rows, :] = done.T.astype(jnp.bfloat16)

    if last:
        for e in range(RING):
            for d in range(RING):
                slot = e * RING + d
                along = place_ref[0] ^ d
                across = place_ref[1] ^ e
                result[along * place_ref[2] + across * place_ref[3]] = q_all[slot * nr : (slot + 1) * nr]


def attend(place, parts, q_from, key_from, groups, acc=None, last=False):
    nq = len(q_from) * RING * QROWS
    total = sum(RING * nk for _, _, _, nk in key_from)
    before = 0 if acc is None else acc.shape[2] // BLOCK_Q
    operands = list(parts) + ([] if acc is None else [acc])
    vmem = pl.BlockSpec(memory_space=pltpu.VMEM)
    if last:
        out_shape = jax.ShapeDtypeStruct((RING * RING, QROWS, PAIR), jnp.bfloat16)
    else:
        out_shape = jax.ShapeDtypeStruct((2, HEAD_DIM + 8, nq), jnp.float32)
    keys = sum(high - low for low, high in groups)
    return pl.pallas_call(
        functools.partial(attend_kernel, len(parts), q_from, key_from, groups, before, last),
        in_specs=[pl.BlockSpec(memory_space=pltpu.SMEM)] + [vmem] * len(operands),
        out_specs=vmem,
        out_shape=out_shape,
        scratch_shapes=[
            pltpu.VMEM((nq, PAIR), jnp.bfloat16),
            pltpu.VMEM((total, PAIR), jnp.bfloat16),
            pltpu.VMEM((VROWS, total), jnp.bfloat16),
            pltpu.VMEM((VROWS, total), jnp.bfloat16),
        ],
        compiler_params=pltpu.CompilerParams(vmem_limit_bytes=32 * MIB),
        cost_estimate=pl.CostEstimate(
            flops=2 * 2 * 4 * BLOCK_Q * keys * PAIR, bytes_accessed=2 * MIB, transcendentals=2 * BLOCK_Q * keys
        ),
        name="attend",
    )(place, *operands)


def project_kernel(place_ref, level_ref, got_ref, hidden_ref, w_proj_ref, w_final_ref, base_ref, slope_ref, *refs):
    velocity_ref, drift_ref, joined = refs
    for j in range(RING * RING):
        hi, lo = divmod(j, RING)
        pair = hi * place_ref[2] + lo * place_ref[3]
        joined[:, pl.ds(pl.multiple_of(pair * PAIR, PAIR), PAIR)] = got_ref[j]
    squares = jnp.zeros((QROWS, 1), jnp.float32)
    product = jnp.zeros((LAT, QROWS), jnp.float32)
    for start, size in cuts_of(D, 512):
        cols = slice(start, start + size)
        projected = jnp.dot(joined[...], w_proj_ref[:, cols], preferred_element_type=jnp.float32)
        gate = base_ref[:, cols] + level_ref[0] * slope_ref[:, cols]
        value = hidden_ref[:, cols].astype(jnp.float32) + gate * projected
        product = product + lax.dot_general(
            w_final_ref[:, cols], value.astype(jnp.bfloat16), NT, preferred_element_type=jnp.float32
        )
        squares = squares + jnp.sum(value * value, axis=1, keepdims=True)
    along = jnp.broadcast_to(squares, (QROWS, PAIR)).T[0:1]
    velocity = product * lax.rsqrt(along * (1.0 / D) + 1e-06)
    velocity_ref[...] = velocity
    drift = velocity * level_ref[1]
    drift_ref[...] = drift


def project(place, level, got, hidden, w_proj, w_final, base, slope):
    vmem = pl.BlockSpec(memory_space=pltpu.VMEM)
    smem = pl.BlockSpec(memory_space=pltpu.SMEM)
    return pl.pallas_call(
        project_kernel,
        in_specs=[smem, smem] + [vmem] * 6,
        out_specs=[vmem] * 2,
        out_shape=[
            jax.ShapeDtypeStruct((LAT, QROWS), jnp.float32),
            jax.ShapeDtypeStruct((LAT, QROWS), jnp.float32),
        ],
        scratch_shapes=[pltpu.VMEM((QROWS, HD), jnp.bfloat16)],
        compiler_params=pltpu.CompilerParams(vmem_limit_bytes=16 * MIB),
        cost_estimate=pl.CostEstimate(flops=2 * QROWS * HD * D, bytes_accessed=12 * MIB, transcendentals=0),
        name="project",
    )(place, level, got, hidden, w_proj, w_final, base, slope)


def sigma_of(index_val, total_steps):
    frac = 1.0 - index_val.astype(jnp.float32) / total_steps
    return 3.0 * frac / (1.0 + 2.0 * frac)


def per_device(
    queries, keys, values, hidden, w_proj, w_final, gate_base, gate_slope, start_latent, window_steps
):
    slots = lax.axis_size("tm")
    slot = lax.axis_index("tm")
    seat = lax.axis_index("seq")
    x, z = seat // RING, lax.rem(seat, RING)
    even = lax.rem(slot, 2) == 0
    first, second = jnp.where(even, x, z), jnp.where(even, z, x)
    place = jnp.stack([first, second, jnp.where(even, RING, 1), jnp.where(even, 1, RING), slot]).astype(jnp.int32)
    sigma_now = sigma_of(window_steps[slot], 2 * slots)
    step_size = sigma_of(window_steps[slot + 1], 2 * slots) - sigma_now
    level = jnp.stack([sigma_now, step_size])

    places, end = layout()
    starts = [0] + [kp for kp, _ in places[1:]] + [end]
    landed = first_hop(queries[0], keys[0], values[0])
    received = [second_hop(landed, start, stop) for start, stop in zip(starts, starts[1:])]
    (a0, a1), (b0, b1) = KEY_CUTS
    na, nb = a1 - a0, b1 - b0
    kb, vb = places[1][0] - starts[1], places[1][1] - starts[1]
    first_part, second_part = received
    in_a = [(e, *places[0], na) for e in range(RING)]
    acc = attend(
        place,
        [first_part[0], first_part[1], second_part[0]],
        (0, 1),
        (*in_a[:2], (2, kb, vb, nb)),
        ((0, RING * (2 * na + nb)),),
    )
    acc = attend(
        place, first_part, range(RING), in_a, ((2 * RING * na, RING * RING * na), (0, RING * RING * na)), acc
    )
    got = attend(
        place,
        [*first_part, *second_part],
        range(RING),
        [(RING + e, kb, vb, nb) for e in range(RING)],
        ((RING * nb, RING * RING * nb), (0, RING * RING * nb)),
        acc,
        True,
    )
    ahead = (lax.broadcasted_iota(jnp.int32, (SLOTS // 2, LAT, QROWS), 0) > slot // 2).astype(jnp.float32)
    from_other = jnp.broadcast_to(jnp.where(even, 0.0, 1.0), (LAT, QROWS))
    got, ahead, from_other, *operands = lax.optimization_barrier(
        (got, ahead, from_other, level, hidden[0], w_proj, w_final.T, gate_base[None], gate_slope[None])
    )
    got = lax.all_to_all(got, "seq", 0, 0, tiled=True)
    velocity, drift = project(place, operands[0], got, *operands[1:])
    other = lax.ppermute(drift, "tm", [(i, i ^ 1) for i in range(SLOTS)])
    later = (ahead * (drift + other)[None]).astype(jnp.bfloat16)
    groups = [[core + 2 * chip for chip in range(SLOTS // 2)] for core in range(2)]
    earlier = lax.all_to_all(later, "tm", 0, 0, axis_index_groups=groups, tiled=True).astype(jnp.float32)
    latents = start_latent.T + drift + from_other * other + jnp.sum(earlier, axis=0)
    return (velocity.T[None], latents.T[None])


def solution(mesh):
    placed = (
        P("tm", "seq", None),
        P("tm", "seq", None),
        P("tm", "seq", None),
        P("tm", "seq", None),
        P(),
        P(),
        P(),
        P(),
        P("seq", None),
        P(),
    )
    return jax.shard_map(
        per_device,
        mesh=mesh,
        in_specs=placed,
        out_specs=(P("tm", "seq", None), P("tm", "seq", None)),
        check_vma=False,
    )
```

```python
import functools

import jax
import jax.numpy as jnp
from jax import lax
from jax.experimental import pallas as pl
from jax.experimental.pallas import tpu as pltpu
from jax.sharding import PartitionSpec as P

HEADS = 32
HEAD_DIM = 64
HD = 2048
D = 2432
LAT = 64
PAIR = 128
RING = 4
SLOTS = 8
BOTH = ("tm", "seq")
NT = (((1,), (1,)), ((), ()))
SCALE = 0.125 * 1.4426950408889634
KEY_CUTS = ((0, 96), (96, 280))
QROWS = 256
KROWS = 280
TILE = 512
BLOCK_Q = 2048
STEP_Q = 1024
VROWS = 128
MIB = 2**20


def swap_pairs(first, mask):
    pairs = []
    for slot in range(8):
        for place in range(16):
            x, z = divmod(place, RING)
            if (slot % 2 == 0) == first:
                x2, z2 = x ^ mask, z
            else:
                x2, z2 = x, z ^ mask
            pairs.append((slot * 16 + place, slot * 16 + x2 * RING + z2))
    return pairs


def send(value, first, mask):
    return lax.ppermute(value, BOTH, swap_pairs(first, mask))


def head_norm(block):
    wide = block.astype(jnp.float32)
    square = wide * wide
    high = square.astype(jnp.bfloat16)
    low = (square - high.astype(jnp.float32)).astype(jnp.bfloat16)
    row = lax.broadcasted_iota(jnp.int32, (PAIR, PAIR), 0)
    col = lax.broadcasted_iota(jnp.int32, (PAIR, PAIR), 1)
    same = ((row < HEAD_DIM) == (col < HEAD_DIM)).astype(jnp.bfloat16)
    total = jnp.dot(high, same, preferred_element_type=jnp.float32)
    total = total + jnp.dot(low, same, preferred_element_type=jnp.float32)
    return (wide * lax.rsqrt(total * (1.0 / HEAD_DIM) + 1e-06)).astype(jnp.bfloat16)


def padded(rows):
    return -(-rows // 16) * 16


def layout():
    at, places = QROWS, []
    for k0, k1 in KEY_CUTS:
        places.append((at, at + padded(k1 - k0)))
        at += 2 * padded(k1 - k0)
    return places, at


def pack_kernel(shifts, q_hbm, k_hbm, v_hbm, *refs):
    seat, odd = lax.axis_index("seq"), lax.rem(lax.axis_index("tm"), 2)
    x, z = seat // RING, lax.rem(seat, RING)
    first, second = x + odd * (z - x), z + odd * (x - z)
    outs, (q_buf, k_buf, v_buf, sems) = refs[: len(shifts)], refs[len(shifts) :]
    places, _ = layout()
    copies = []
    for i, d in enumerate(shifts):
        group = first ^ d
        lanes = pl.ds(pl.multiple_of(group * (RING * PAIR), RING * PAIR), RING * PAIR)
        copies.append(
            [
                pltpu.make_async_copy(source.at[:, lanes], target.at[i], sems.at[i, n])
                for n, (source, target) in enumerate(((q_hbm, q_buf), (k_hbm, k_buf), (v_hbm, v_buf)))
            ]
        )
        for copy in copies[i]:
            copy.start()
    for i in range(len(shifts)):
        for copy in copies[i]:
            copy.wait()
        out = outs[i]
        for e in range(RING):
            pair = second ^ e
            lanes = pl.ds(pl.multiple_of(pair * PAIR, PAIR), PAIR)
            out[e, 0:QROWS] = head_norm(q_buf[i, :, lanes])
            keys = head_norm(k_buf[i, :, lanes])
            for (k0, k1), (kp, vp) in zip(KEY_CUTS, places):
                out[e, kp : kp + k1 - k0] = keys[k0:k1]
                out[e, vp : vp + k1 - k0] = v_buf[i, k0:k1, lanes]
                gap = padded(k1 - k0) - (k1 - k0)
                if gap:
                    out[e, vp - gap : vp] = jnp.zeros((gap, PAIR), jnp.bfloat16)
                    out[e, vp + k1 - k0 : vp + k1 - k0 + gap] = jnp.zeros((gap, PAIR), jnp.bfloat16)


def pack(queries, keys, values, shifts):
    _, rows = layout()
    vmem = pl.BlockSpec(memory_space=pltpu.VMEM)
    wide = RING * PAIR
    count = len(shifts)
    return pl.pallas_call(
        functools.partial(pack_kernel, shifts),
        in_specs=[pl.BlockSpec(memory_space=pltpu.HBM)] * 3,
        out_specs=[vmem] * count,
        out_shape=[jax.ShapeDtypeStruct((RING, rows, PAIR), jnp.bfloat16)] * count,
        scratch_shapes=[
            pltpu.VMEM((count, QROWS, wide), jnp.bfloat16),
            pltpu.VMEM((count, KROWS, wide), jnp.bfloat16),
            pltpu.VMEM((count, KROWS, wide), jnp.bfloat16),
            pltpu.SemaphoreType.DMA((count, 3)),
        ],
        compiler_params=pltpu.CompilerParams(vmem_limit_bytes=59 * MIB),
        cost_estimate=pl.CostEstimate(
            flops=count * rows * HD * PAIR, bytes_accessed=count * rows * HD, transcendentals=0
        ),
        name="pack",
    )(queries, keys, values)


def first_hop(queries, keys, values):
    up, down, across, own = pack(queries, keys, values, (1, 3, 2, 0))
    return [own, send(up, True, 1), send(across, True, 2), send(down, True, 3)]


def second_hop(landed, start, stop):
    staged = [jnp.stack([part[e, start:stop] for part in landed]) for e in range(RING)]
    return [staged[0]] + [send(staged[e], False, e) for e in range(1, RING)]


def cuts_of(total, step):
    return [(start, min(step, total - start)) for start in range(0, total, step)]


def attend_kernel(count, q_from, key_from, groups, before, last, place_ref, *refs):
    parts, refs = refs[:count], refs[count:]
    if before:
        acc, refs = refs[0], refs[1:]
    result, q_all, k_all, low_t, high_t = refs
    nr = QROWS
    row = lax.broadcasted_iota(jnp.int32, (PAIR, PAIR), 0)
    col = lax.broadcasted_iota(jnp.int32, (PAIR, PAIR), 1)
    eye = (row == col).astype(jnp.bfloat16)
    for i, source in enumerate(q_from):
        for d in range(RING):
            slot = i * RING + d
            q_all[slot * nr : (slot + 1) * nr] = parts[source][d, 0:nr]
    low_t[HEAD_DIM:, :] = jnp.ones((VROWS - HEAD_DIM, low_t.shape[1]), jnp.bfloat16)
    high_t[HEAD_DIM:, :] = jnp.ones((VROWS - HEAD_DIM, low_t.shape[1]), jnp.bfloat16)
    at = 0
    for source, kp, vp, nk in key_from:
        part = parts[source]
        for d in range(RING):
            k_all[at + d * nk : at + (d + 1) * nk] = part[d, kp : kp + nk]
        joined = jnp.concatenate([part[d, vp : vp + nk] for d in range(RING)], axis=0)
        turned = lax.dot_general(eye, joined, NT, preferred_element_type=jnp.float32).astype(jnp.bfloat16)
        low_t[0:HEAD_DIM, at : at + RING * nk] = turned[:HEAD_DIM]
        high_t[0:HEAD_DIM, at : at + RING * nk] = turned[HEAD_DIM:]
        at += RING * nk
    values_t = (low_t, high_t)
    kept = HEAD_DIM + 8
    step_q = BLOCK_Q if last else STEP_Q
    for block, (lowest, highest) in enumerate(groups):
        work = [(h, lowest + start, size) for start, size in cuts_of(highest - lowest, TILE) for h in range(2)]

        @pl.loop(0, BLOCK_Q // step_q)
        def _(step, block=block, work=work):
            rows = pl.ds(pl.multiple_of(block * BLOCK_Q + step * step_q, step_q), step_q)
            q = q_all[rows, :]
            lane = lax.broadcasted_iota(jnp.int32, q.shape, 1)
            zero = jnp.zeros_like(q)
            halves = (jnp.where(lane < HEAD_DIM, q, zero), jnp.where(lane < HEAD_DIM, zero, q))
            sums = [jnp.zeros((VROWS, step_q), jnp.float32) for _ in range(2)]

            def score(item):
                h, start, size = item
                return lax.dot_general(
                    k_all[start : start + size, :], halves[h], NT, preferred_element_type=jnp.float32
                )

            ahead = score(work[0])
            for i, (h, start, size) in enumerate(work):
                now = ahead
                if i + 1 < len(work):
                    ahead = score(work[i + 1])
                weights = jnp.exp2(now * SCALE).astype(jnp.bfloat16)
                sums[h] = sums[h] + jnp.dot(
                    values_t[h][:, start : start + size], weights, preferred_element_type=jnp.float32
                )
            sums = [part[:kept] for part in sums]
            if block < before:
                sums = [part + acc[h, :, rows] for h, part in enumerate(sums)]
            if not last:
                for h in range(2):
                    result[h, :, rows] = sums[h]
            else:
                done = jnp.concatenate([part[:HEAD_DIM] / part[HEAD_DIM : HEAD_DIM + 1] for part in sums], axis=0)
                q_all[rows, :] = done.T.astype(jnp.bfloat16)

    if last:
        for e in range(RING):
            for d in range(RING):
                slot = e * RING + d
                along = place_ref[0] ^ d
                across = place_ref[1] ^ e
                result[along * place_ref[2] + across * place_ref[3]] = q_all[slot * nr : (slot + 1) * nr]


def attend(place, parts, q_from, key_from, groups, acc=None, last=False):
    nq = len(q_from) * RING * QROWS
    total = sum(RING * nk for _, _, _, nk in key_from)
    before = 0 if acc is None else acc.shape[2] // BLOCK_Q
    operands = list(parts) + ([] if acc is None else [acc])
    vmem = pl.BlockSpec(memory_space=pltpu.VMEM)
    if last:
        out_shape = jax.ShapeDtypeStruct((RING * RING, QROWS, PAIR), jnp.bfloat16)
    else:
        out_shape = jax.ShapeDtypeStruct((2, HEAD_DIM + 8, nq), jnp.float32)
    keys = sum(high - low for low, high in groups)
    return pl.pallas_call(
        functools.partial(attend_kernel, len(parts), q_from, key_from, groups, before, last),
        in_specs=[pl.BlockSpec(memory_space=pltpu.SMEM)] + [vmem] * len(operands),
        out_specs=vmem,
        out_shape=out_shape,
        scratch_shapes=[
            pltpu.VMEM((nq, PAIR), jnp.bfloat16),
            pltpu.VMEM((total, PAIR), jnp.bfloat16),
            pltpu.VMEM((VROWS, total), jnp.bfloat16),
            pltpu.VMEM((VROWS, total), jnp.bfloat16),
        ],
        compiler_params=pltpu.CompilerParams(vmem_limit_bytes=32 * MIB),
        cost_estimate=pl.CostEstimate(
            flops=2 * 2 * 4 * BLOCK_Q * keys * PAIR, bytes_accessed=2 * MIB, transcendentals=2 * BLOCK_Q * keys
        ),
        name="attend",
    )(place, *operands)


def project_kernel(place_ref, level_ref, got_ref, hidden_ref, w_proj_ref, w_final_ref, base_ref, slope_ref, *refs):
    velocity_ref, drift_ref, joined = refs
    for j in range(RING * RING):
        hi, lo = divmod(j, RING)
        pair = hi * place_ref[2] + lo * place_ref[3]
        joined[:, pl.ds(pl.multiple_of(pair * PAIR, PAIR), PAIR)] = got_ref[j]
    squares = jnp.zeros((QROWS, 1), jnp.float32)
    product = jnp.zeros((LAT, QROWS), jnp.float32)
    for start, size in cuts_of(D, 512):
        cols = slice(start, start + size)
        projected = jnp.dot(joined[...], w_proj_ref[:, cols], preferred_element_type=jnp.float32)
        gate = base_ref[:, cols] + level_ref[0] * slope_ref[:, cols]
        value = hidden_ref[:, cols].astype(jnp.float32) + gate * projected
        product = product + lax.dot_general(
            w_final_ref[:, cols], value.astype(jnp.bfloat16), NT, preferred_element_type=jnp.float32
        )
        squares = squares + jnp.sum(value * value, axis=1, keepdims=True)
    along = jnp.broadcast_to(squares, (QROWS, PAIR)).T[0:1]
    velocity = product * lax.rsqrt(along * (1.0 / D) + 1e-06)
    velocity_ref[...] = velocity
    drift = velocity * level_ref[1]
    drift_ref[...] = drift


def project(place, level, got, hidden, w_proj, w_final, base, slope):
    vmem = pl.BlockSpec(memory_space=pltpu.VMEM)
    smem = pl.BlockSpec(memory_space=pltpu.SMEM)
    return pl.pallas_call(
        project_kernel,
        in_specs=[smem, smem] + [vmem] * 6,
        out_specs=[vmem] * 2,
        out_shape=[
            jax.ShapeDtypeStruct((LAT, QROWS), jnp.float32),
            jax.ShapeDtypeStruct((LAT, QROWS), jnp.float32),
        ],
        scratch_shapes=[pltpu.VMEM((QROWS, HD), jnp.bfloat16)],
        compiler_params=pltpu.CompilerParams(vmem_limit_bytes=16 * MIB),
        cost_estimate=pl.CostEstimate(flops=2 * QROWS * HD * D, bytes_accessed=12 * MIB, transcendentals=0),
        name="project",
    )(place, level, got, hidden, w_proj, w_final, base, slope)


def sigma_of(index_val, total_steps):
    frac = 1.0 - index_val.astype(jnp.float32) / total_steps
    return 3.0 * frac / (1.0 + 2.0 * frac)


def per_device(
    queries, keys, values, hidden, w_proj, w_final, gate_base, gate_slope, start_latent, window_steps
):
    slots = lax.axis_size("tm")
    slot = lax.axis_index("tm")
    seat = lax.axis_index("seq")
    x, z = seat // RING, lax.rem(seat, RING)
    even = lax.rem(slot, 2) == 0
    first, second = jnp.where(even, x, z), jnp.where(even, z, x)
    place = jnp.stack([first, second, jnp.where(even, RING, 1), jnp.where(even, 1, RING), slot]).astype(jnp.int32)
    sigma_now = sigma_of(window_steps[slot], 2 * slots)
    step_size = sigma_of(window_steps[slot + 1], 2 * slots) - sigma_now
    level = jnp.stack([sigma_now, step_size])

    places, end = layout()
    starts = [0] + [kp for kp, _ in places[1:]] + [end]
    landed = first_hop(queries[0], keys[0], values[0])
    received = [second_hop(landed, start, stop) for start, stop in zip(starts, starts[1:])]
    (a0, a1), (b0, b1) = KEY_CUTS
    na, nb = a1 - a0, b1 - b0
    kb, vb = places[1][0] - starts[1], places[1][1] - starts[1]
    first_part, second_part = received
    in_a = [(e, *places[0], na) for e in range(RING)]
    acc = attend(
        place,
        [first_part[0], first_part[1], second_part[0]],
        (0, 1),
        (*in_a[:2], (2, kb, vb, nb)),
        ((0, RING * (2 * na + nb)),),
    )
    acc = attend(
        place, first_part, range(RING), in_a, ((2 * RING * na, RING * RING * na), (0, RING * RING * na)), acc
    )
    got = attend(
        place,
        [*first_part, *second_part],
        range(RING),
        [(RING + e, kb, vb, nb) for e in range(RING)],
        ((RING * nb, RING * RING * nb), (0, RING * RING * nb)),
        acc,
        True,
    )
    ahead = (lax.broadcasted_iota(jnp.int32, (SLOTS // 2, LAT, QROWS), 0) > slot // 2).astype(jnp.float32)
    from_other = jnp.broadcast_to(jnp.where(even, 0.0, 1.0), (LAT, QROWS))
    got, ahead, from_other, *operands = lax.optimization_barrier(
        (got, ahead, from_other, level, hidden[0], w_proj, w_final.T, gate_base[None], gate_slope[None])
    )
    got = lax.all_to_all(got, "seq", 0, 0, tiled=True)
    velocity, drift = project(place, operands[0], got, *operands[1:])
    other = lax.ppermute(drift, "tm", [(i, i ^ 1) for i in range(SLOTS)])
    later = (ahead * (drift + other)[None]).astype(jnp.bfloat16)
    groups = [[core + 2 * chip for chip in range(SLOTS // 2)] for core in range(2)]
    earlier = lax.all_to_all(later, "tm", 0, 0, axis_index_groups=groups, tiled=True).astype(jnp.float32)
    latents = start_latent.T + drift + from_other * other + jnp.sum(earlier, axis=0)
    return (velocity.T[None], latents.T[None])


def solution(mesh):
    placed = (
        P("tm", "seq", None),
        P("tm", "seq", None),
        P("tm", "seq", None),
        P("tm", "seq", None),
        P(),
        P(),
        P(),
        P(),
        P("seq", None),
        P(),
    )
    return jax.shard_map(
        per_device,
        mesh=mesh,
        in_specs=placed,
        out_specs=(P("tm", "seq", None), P("tm", "seq", None)),
        check_vma=False,
    )
```
